32 devices in a mesh: group: 4 (over y, x), sector: 8 (over z, core).
Axes of the slice: x: 2, y: 2, z: 4, core: 2. Of those that a mesh axis runs over, the one named last changes fastest.
Arguments:
- state: float32 [32, 128, 4, 128], P(('group', 'sector')), may hold values from -180 to 180
- panel: bfloat16 [32, 32, 256], P('group'), may hold values from -3 to 3
- left_env: bfloat16 [32, 32, 128, 128], P(('group', 'sector')), may hold values from -1.5 to 1.5
- right_env: bfloat16 [32, 32, 128, 128], P(('group', 'sector')), may hold values from -1 to 1
- left_match: int32 [32], P(('group', 'sector')), may hold values from 0 to 7
- right_match: int32 [32], P(('group', 'sector')), may hold values from 0 to 7
- phys_states: int32 [32, 4], P(('group', 'sector')), may hold values from 0 to 15, all different within a row
Outputs:
- new_state: float32 [32, 128, 4, 128], P(('group', 'sector'))
- hessenberg: float32 [8, 8], replicated
The draws below stay inside these ranges and needn't reach their ends.
Inputs may be any that keep to these rules, and one draw needn't show every extreme that they name: `left_match`: environment block index within the sector's own group, below 8. `right_match`: environment block index within the sector's own group, below 8. `phys_states`: each sector's 4 states are different.
All inputs are finite; a program needn't handle non-finite values.
Results may differ from the reference program's by a relative error of at most 0.025.
Values may be sent and summed in bfloat16 or wider, within the bound.
No kernel may reach another device: no remote copies, remote signals or barrier semaphores. Data moves between devices by JAX's collectives and lax.ppermute only.
A program may use at most 128 MiB of HBM per device.

```python
import math
import jax
import jax.numpy as jnp
import numpy as np
from jax import lax

CHANNELS = 32
BLOCK = 128
PHYS = 4
LOCAL = 16
KRYLOV = 8
SECTORS = 32
ENV_GRP = 8


def draw_state(key, part):
    key = jax.random.fold_in(key, 11)
    first_key, row_key, col_key = jax.random.split(key, 3)
    shape = (SECTORS, BLOCK, PHYS, BLOCK)
    rising = 1.0 + 2.0 * jnp.arange(SECTORS, dtype=jnp.float32) / max(SECTORS - 1, 1)
    rising = rising.reshape(SECTORS, 1, 1, 1)
    row_scale = jnp.exp(jax.random.uniform(row_key, (SECTORS, BLOCK, 1, 1)) * math.log(10.0))
    col_scale = jnp.exp(jax.random.uniform(col_key, (SECTORS, 1, 1, BLOCK)) * math.log(10.0))
    base_draw = jnp.clip(jax.random.normal(first_key, shape), -6.0, 6.0)
    return (base_draw * rising * row_scale * col_scale / 10.0).astype(jnp.float32)


def unit_noise(key, shape, limit):
    return jnp.clip(jax.random.normal(key, shape), -limit, limit)


def draw_panel(key, part):
    key = jax.random.fold_in(key, 21)
    noise_key, jitter_key, repulse_key, chem_key = jax.random.split(key, 4)
    shape = (CHANNELS, CHANNELS, LOCAL * LOCAL)
    values = unit_noise(noise_key, shape, 6.0) * (CHANNELS * PHYS) ** (-0.5)
    repulsion = jax.random.uniform(repulse_key, (), minval=1.0, maxval=2.0)
    chemical = jax.random.uniform(chem_key, (), minval=0.4, maxval=0.8)
    site_state = jnp.arange(LOCAL, dtype=jnp.int32)
    first_site = site_state // 4
    second_site = site_state % 4
    filling = (first_site > 0).astype(jnp.float32) + (first_site == 3).astype(jnp.float32) + (second_site > 0).astype(jnp.float32) + (second_site == 3).astype(jnp.float32)
    doubles = (first_site == 3).astype(jnp.float32) + (second_site == 3).astype(jnp.float32)
    jitter = 0.2 * jnp.clip(jax.random.normal(jitter_key, (LOCAL,)), -3.0, 3.0)
    energy = repulsion * doubles - chemical * filling + jitter
    pair_ids = jnp.arange(LOCAL * LOCAL, dtype=jnp.int32)
    onsite = jnp.where(pair_ids // LOCAL == pair_ids % LOCAL, energy[pair_ids // LOCAL], 0.0)
    values = values.at[0, CHANNELS - 1].set(onsite)
    return values.astype(jnp.bfloat16)


def draw_left_env(key, part):
    key = jax.random.fold_in(key, 31)
    shape = (SECTORS, CHANNELS, BLOCK, BLOCK)
    values = unit_noise(key, shape, 4.0) * BLOCK ** (-0.5)
    identity = jnp.broadcast_to(jnp.eye(BLOCK, dtype=jnp.float32), (SECTORS, BLOCK, BLOCK))
    values = values.at[:, 0].set(identity)
    return values.astype(jnp.bfloat16)


def draw_right_env(key, part):
    key = jax.random.fold_in(key, 41)
    shape = (SECTORS, CHANNELS, BLOCK, BLOCK)
    values = unit_noise(key, shape, 6.0) * (CHANNELS * BLOCK) ** (-0.5)
    identity = jnp.broadcast_to(jnp.eye(BLOCK, dtype=jnp.float32), (SECTORS, BLOCK, BLOCK))
    values = values.at[:, CHANNELS - 1].set(identity)
    return values.astype(jnp.bfloat16)


def plant(array, own_key, smallest, high):
    dims = array.shape
    index_at = [jax.random.randint(jax.random.fold_in(own_key, axis), (), 0, dims[axis]) for axis in range(len(dims))]
    array = array.at[tuple(index_at)].set(smallest)
    longest = dims.index(max(dims))
    index_at[longest] = (index_at[longest] + 1) % dims[longest]
    return array.at[tuple(index_at)].set(high)


def rank_table(count, skew):
    weights = [(1 << 20) // math.isqrt(standing ** skew) + 1 for standing in range(1, count + 1)]
    width = 1 + sum(weights) // (1 << 30)
    return np.cumsum(np.array([max(1, weight // width) for weight in weights]))


def skewed_ids(rng, extent, number_of, lean):
    listing = rank_table(number_of, lean)
    ticket = jax.random.randint(jax.random.fold_in(rng, 1), extent, 0, int(listing[number_of - 1]))
    grade = jnp.searchsorted(jnp.asarray(listing, jnp.int32), ticket, side="right")
    return jax.random.permutation(jax.random.fold_in(rng, 2), number_of)[grade].astype(jnp.int32)


def choose_distinct(stream_key, rows, count, top, lift):
    order = jax.random.permutation(jax.random.fold_in(stream_key, 1), count)
    favour = order
    for power in range(3):
        favour = favour * favour // count
    favour = favour * lift // count
    chance = jax.random.randint(jax.random.fold_in(stream_key, 2), (rows, count), 0, 4096) + favour
    sure = jax.random.permutation(jax.random.fold_in(stream_key, 3), rows)[jnp.arange(count) % rows]
    chance = jnp.where(jnp.arange(rows)[:, None] == sure[None, :], 1 << 14, chance)
    priority = chance * count + jnp.arange(count)
    return lax.top_k(priority.astype(jnp.int32), top)[1].astype(jnp.int32)


def setup_inputs(seed: int = 0) -> dict:
    seeds = jax.random.split(jax.random.key(seed), 8)
    return {
        "state": draw_state(jax.random.fold_in(seeds[7], 71), 0),
        "panel": draw_panel(jax.random.fold_in(seeds[7], 71), 0),
        "left_env": draw_left_env(jax.random.fold_in(seeds[7], 71), 0),
        "right_env": draw_right_env(jax.random.fold_in(seeds[7], 71), 0),
        "left_match": plant(skewed_ids(seeds[4], (SECTORS,), ENV_GRP, 2), jax.random.fold_in(seeds[4], 3), 0, ENV_GRP - 1).astype(jnp.int32),
        "right_match": plant(skewed_ids(seeds[5], (SECTORS,), ENV_GRP, 1), jax.random.fold_in(seeds[5], 3), 0, ENV_GRP - 1).astype(jnp.int32),
        "phys_states": choose_distinct(seeds[6], SECTORS, LOCAL, PHYS, 0),
    }


TAU = 3.0
EPS = 1e-06
HIGH = lax.Precision.HIGHEST

def select_mix(panel, states):
    pairs = states[:, None] * 16 + states[None, :]
    choose = (jnp.arange(panel.shape[2], dtype=jnp.int32)[None, None, :] == pairs[:, :, None]).astype(jnp.float32)
    mixed = jnp.einsum('acz,qpz->aqcp', panel.astype(jnp.float32), choose, precision=HIGH)
    return mixed.astype(jnp.bfloat16)

def apply_sector(block_in, left_block, right_block, mixing):
    channels, size = (left_block.shape[0], left_block.shape[1])
    states = block_in.shape[1]
    inner = jnp.dot(left_block.reshape(channels * size, size), block_in.reshape(size, states * size), preferred_element_type=jnp.float32)
    inner = inner.astype(jnp.bfloat16).reshape(channels, size, states, size)
    middle = jnp.einsum('aiqj,aqcp->cipj', inner.astype(jnp.float32), mixing.astype(jnp.float32)).astype(jnp.bfloat16)
    return jnp.einsum('cipj,crj->ipr', middle.astype(jnp.float32), right_block.astype(jnp.float32))

def exponent_column(hessenberg):
    scaled = -TAU / 16.0 * hessenberg
    power_term = jnp.eye(hessenberg.shape[0], dtype=jnp.float32)
    series = power_term
    for order in range(1, 11):
        power_term = jnp.dot(power_term, scaled, precision=HIGH) / float(order)
        series = series + power_term
    for square in range(4):
        series = jnp.dot(series, series, precision=HIGH)
    return series[:, 0]

def reference(state, panel, left_env, right_env, left_match, right_match, phys_states):
    sector_ids = jnp.arange(SECTORS, dtype=jnp.int32)
    group_base = sector_ids // ENV_GRP * ENV_GRP
    left_ids = (group_base + left_match).astype(jnp.int32)
    right_ids = (group_base + right_match).astype(jnp.int32)
    mixes = jax.vmap(lambda states: select_mix(panel, states))(phys_states)

    def operate(vector):
        blocks = vector.reshape(SECTORS, BLOCK, PHYS, BLOCK).astype(jnp.bfloat16)

        def one_sector(pieces):
            block_in, left_id, right_id, mixing = pieces
            left_block = lax.dynamic_index_in_dim(left_env, left_id, 0, keepdims=False)
            right_block = lax.dynamic_index_in_dim(right_env, right_id, 0, keepdims=False)
            return apply_sector(block_in, left_block, right_block, mixing)
        return lax.map(one_sector, (blocks, left_ids, right_ids, mixes)).reshape(-1)
    flattened = state.reshape(-1)
    length = flattened.shape[0]
    start_sq = jnp.sum(flattened * flattened)
    krylov_basis = jnp.zeros((KRYLOV, length), jnp.float32).at[0].set(flattened / jnp.sqrt(start_sq + EPS))
    hessenberg = jnp.zeros((KRYLOV, KRYLOV), jnp.float32)
    for column in range(KRYLOV):
        applied = operate(krylov_basis[column])
        projection = jnp.dot(krylov_basis, applied, precision=HIGH)
        remainder = applied - jnp.dot(projection, krylov_basis, precision=HIGH)
        hessenberg = hessenberg.at[:, column].set(projection)
        if column + 1 < KRYLOV:
            subdiag = jnp.sqrt(jnp.sum(remainder * remainder) + EPS)
            hessenberg = hessenberg.at[column + 1, column].set(subdiag)
            krylov_basis = krylov_basis.at[column + 1].set(remainder / subdiag)
    coefficients = exponent_column(hessenberg)
    rescale = jnp.sqrt(jnp.float32(length)) / jnp.sqrt(jnp.sum(coefficients * coefficients))
    evolved = jnp.dot(coefficients, krylov_basis, precision=HIGH) * rescale
    return (evolved.reshape(state.shape), hessenberg)
```

```python
import jax
import jax.numpy as jnp
from jax import lax
from jax.experimental import pallas as pl
from jax.experimental.pallas import tpu as pltpu
from jax.sharding import PartitionSpec as P

KRYLOV = 8
LOCAL = 16
TAU = 3.0
EPS = 1e-06
TINY = 1e-30
LANES = 128
STREAMS = 2
OWN = 4
FIXED_ROUNDS = 5
TAIL_ROUNDS = 7
SLOTS = 64
LINE = 4


def spread_rows(x, axis, combine, fallback):
    count = lax.axis_size(axis)
    if count & (count - 1):
        return fallback(x, axis)
    while count > 1:
        radix = 4 if count % 4 == 0 else 2
        count //= radix
        size = lax.axis_size(axis)
        others = [
            lax.ppermute(x, axis, [(k, k ^ (count * turn)) for k in range(size)])
            for turn in range(1, radix)
        ]
        for other in others:
            x = combine(x, other)
    return x


def select_mix(slices, states):
    pairs = states[:, None] * LOCAL + states[None, :]
    choose = (
        jnp.arange(slices[0].shape[2], dtype=jnp.int32)[None, None, :] == pairs[:, :, None]
    ).astype(jnp.bfloat16)
    panel = jnp.concatenate(slices, axis=0)
    mixed = jnp.einsum("acz,qpz->cpqa", panel, choose, preferred_element_type=jnp.float32)
    return mixed.astype(jnp.bfloat16)


def arrange_mix(mixed, share):
    group = lax.axis_size("group")
    turned = (group - lax.axis_index("group")) % group * share
    mixed = lax.dynamic_slice_in_dim(
        jnp.concatenate([mixed, mixed], axis=3), turned, mixed.shape[3], axis=3
    )
    channels, phys = mixed.shape[0], mixed.shape[1]
    same = jnp.eye(2, dtype=jnp.bfloat16)
    both = mixed[:, None, :, None] * same[None, :, None, :, None, None]
    return both.reshape(channels * 2 * phys, 2 * phys * channels)


def krylov_kernel(table_ref, me_ref, state_ref, mix_ref, theirs_ref, *refs):
    pieces, refs = refs[:-10], refs[-10:]
    basis_ref, stats_ref, mine_ref, wide_ref, rows_ref, turned_ref, x_ref, m_ref, w_ref, sems = refs
    channels, size = theirs_ref.shape[1], theirs_ref.shape[2]
    loads = []
    if pieces:
        loads = [
            held_copies(kind, 0, me_ref, table_ref, pieces, mine_ref.at[kind], sems)
            for kind in range(2)
        ]
        for copies in loads:
            run_copies(copies, "start")
    phys = state_ref.shape[0] // size
    count = basis_ref.shape[0]
    f32, bf16 = jnp.float32, jnp.bfloat16

    def load_left(part):
        def turn(n, carry):
            for k in range(8):
                wide_ref[pl.ds(8 * n + k, size, stride=channels), :] = part[0, 8 * n + k].astype(f32)
            return carry

        lax.fori_loop(0, channels // 8, turn, 0)

    def load_right(part):
        def turn(n, carry):
            for k in range(8):
                at = pl.multiple_of((8 * n + k) * size, size)
                turned_ref[pl.ds(at, size), :] = part[1, 8 * n + k].T
            return carry

        lax.fori_loop(0, channels // 8, turn, 0)

    for kind, load in enumerate((load_left, load_right)):
        here = table_ref[1, kind] >= 0
        if loads:
            run_copies(loads[kind], "wait")

        @pl.when(here)
        def _(load=load):
            load(mine_ref)

        @pl.when(jnp.logical_not(here))
        def _(load=load):
            load(theirs_ref)

    rows_ref[...] = wide_ref[...].astype(bf16)

    basis_ref[...] = jnp.zeros_like(basis_ref)
    start = state_ref[...]
    start_sq = jnp.sum(start * start, keepdims=True)
    start_scale = jnp.sqrt(jnp.maximum(start_sq, TINY))
    basis_ref[0] = start / start_scale

    sub = lax.broadcasted_iota(jnp.int32, (8, LANES), 0)
    lane = lax.broadcasted_iota(jnp.int32, (8, LANES), 1)
    stats = jnp.where((sub == 7) & (lane == 7), start_scale, 0.0)

    group_rows = 4 * channels
    chunk = 64
    once = 64

    def column(j, stats):
        for q in range(phys):
            x_ref[:, q * size : (q + 1) * size] = basis_ref[
                j, pl.ds(q, size, stride=phys), :
            ].astype(bf16)

        def part(n, carry):
            for k in range(chunk // 4):
                if k % (once // 4) == 0:
                    at = n * chunk * channels + k * group_rows
                    at = pl.multiple_of(at, once * channels)
                    z = jnp.dot(
                        rows_ref[pl.ds(at, once * channels), :],
                        x_ref[...],
                        preferred_element_type=f32,
                    ).astype(bf16)
                first = k % (once // 4) * group_rows
                four = z[first : first + group_rows]
                halves = []
                for h in range(2):
                    pieces = []
                    for i2 in range(2):
                        base = (2 * h + i2) * channels
                        for q in range(phys):
                            pieces.append(
                                four[base : base + channels, q * size : (q + 1) * size]
                            )
                    halves.append(jnp.concatenate(pieces, axis=0))
                mixed = jnp.dot(
                    mix_ref[...], jnp.concatenate(halves, axis=1), preferred_element_type=f32
                )
                to = pl.multiple_of(n * chunk * phys, chunk * phys) + k * 4 * phys
                for c in range(channels):
                    block = mixed[c * 2 * phys : (c + 1) * 2 * phys]
                    m_ref[pl.ds(to, 4 * phys), c * size : (c + 1) * size] = jnp.concatenate(
                        [block[:, :size], block[:, size:]], axis=0
                    ).astype(bf16)
            return carry

        lax.fori_loop(0, size // chunk, part, 0)
        step = 64
        half = size * phys // 2
        sums = [jnp.zeros((8, LANES), f32) for _ in range(count + 1)]
        for start in range(0, size * phys, half):
            whole = jnp.dot(
                m_ref[start : start + half, :], turned_ref[...], preferred_element_type=f32
            )
            w_ref[start : start + half, :] = whole
            for at in range(start, start + half, step):
                w = whole[at - start : at - start + step]
                for i in range(count):
                    product = basis_ref[i, at : at + step, :] * w
                    sums[i] = sums[i] + jnp.sum(product.reshape(step // 8, 8, LANES), axis=0)
                sums[count] = sums[count] + jnp.sum((w * w).reshape(step // 8, 8, LANES), axis=0)
        stacked = jnp.zeros((8, LANES), f32)
        for i in range(count):
            stacked = jnp.where(sub == i, jnp.sum(sums[i], axis=0, keepdims=True), stacked)
        h = jnp.sum(stacked, axis=1, keepdims=True)
        w_sq = jnp.sum(sums[count], keepdims=True)
        left_sq = w_sq - jnp.sum(h * h, axis=0, keepdims=True)
        scale = jnp.sqrt(jnp.maximum(jnp.maximum(left_sq, 1e-10 * w_sq), TINY))
        inverse = 1.0 / scale

        @pl.when(j + 1 < count)
        def _():
            for at in range(0, size * phys, step):
                rest = w_ref[at : at + step, :]
                for i in range(count):
                    rest = rest - h[i : i + 1, :] * basis_ref[i, at : at + step, :]
                basis_ref[j + 1, at : at + step, :] = rest * inverse

        entry = jnp.where((sub == j + 1), scale, jnp.broadcast_to(h, (8, LANES)))
        return stats + jnp.where(lane == 8 * j + sub, entry, 0.0)

    stats = lax.fori_loop(0, count, column, stats)

    pairs = [(i, k) for i in range(count) for k in range(i + 1)]

    def gram(r, sums):
        for part in range(4):
            at = pl.multiple_of((4 * r + part) * 8, 8)
            rows = [basis_ref[i, pl.ds(at, 8), :] for i in range(count)]
            sums = [total + rows[i] * rows[k] for total, (i, k) in zip(sums, pairs)]
        return sums

    totals = lax.fori_loop(
        0, size * phys // 32, gram, [jnp.zeros((8, LANES), f32) for _ in pairs]
    )
    for (i, k), total in zip(pairs, totals):
        value = jnp.sum(total, keepdims=True)
        here = (lane == 64 + 8 * i + k) | (lane == 64 + 8 * k + i)
        stats = stats + jnp.where(here & (sub == 0), value, 0.0)
    seats = lax.broadcasted_iota(jnp.int32, stats_ref.shape, 0)
    stats_ref[...] = jnp.where(seats == me_ref[0], jnp.sum(stats, axis=0, keepdims=True), 0.0)


def schedule(origin, reach, own_slot, rows):
    sub = lax.broadcasted_iota(jnp.int32, (rows, LANES), 0)
    lane = lax.broadcasted_iota(jnp.int32, (rows, LANES), 1)
    wanted = (origin <= sub) & (reach > sub)
    score = jnp.where(wanted, (reach * LANES + lane) * SLOTS, -1)
    ready = jnp.where(wanted & (origin == sub), score + own_slot, -1)
    later = jnp.where(origin == sub, -1, score)

    def step(carry, turn):
        ready, later, held, table, used = carry
        best = jnp.max(ready, axis=1, keepdims=True)
        chosen = (ready == best) & (best >= 0)
        table = jnp.where(lane == turn, jnp.where(best >= 0, best & (SLOTS - 1), -1), table)
        used = jnp.where(jnp.max(best, axis=0, keepdims=True) >= 0, turn + 1, used)
        passed = jnp.where(chosen, 1, 0)
        arrived = jnp.concatenate([jnp.zeros((1, LANES), jnp.int32), passed[:-1]], axis=0) > 0
        slot = OWN + turn
        ready = jnp.where(chosen, -1, ready)
        ready = jnp.where(arrived & (later >= 0), later + slot, ready)
        later = jnp.where(arrived, -1, later)
        return ready, later, jnp.where(arrived, slot, held), table, used

    start = jnp.zeros((rows, LANES), jnp.int32)
    return (ready, later, start, start - 1, jnp.zeros((1, 1), jnp.int32)), step


def route_kernel(sectors, where_ref, lists_ref, table_ref, count_ref):
    chips = sectors // 2
    rows = -(-chips // 8) * 8
    lane = lax.broadcasted_iota(jnp.int32, (1, LANES), 1)
    valid = lane < 2 * sectors
    block = lane % sectors
    origin = jnp.where(valid, block // 2, chips)
    own_slot = 2 * (lane // sectors) + block % 2
    reach = jnp.full((1, LANES), -1, jnp.int32)
    back = jnp.full((1, LANES), -1, jnp.int32)
    for k in range(sectors):
        asked = jnp.where(lane < sectors, lists_ref[0, 2 * k], lists_ref[0, 2 * k + 1])
        hit = (block == asked) & valid
        reach = jnp.where(hit, k // 2, reach)
        back = jnp.where(hit, jnp.maximum(back, chips - 1 - k // 2), back)
    right, right_step = schedule(origin, reach, own_slot, rows)
    mirrored = jnp.where(valid, chips - 1 - origin, chips)
    left, left_step = schedule(mirrored, back, own_slot, rows)

    def busy(carry):
        _, right, left = carry
        return jnp.maximum(jnp.max(right[0]), jnp.max(left[0])) >= 0

    def step(carry):
        turn, right, left = carry
        return turn + 1, right_step(right, turn), left_step(left, turn)

    carry = (jnp.int32(0), right, left)
    for _ in range(FIXED_ROUNDS):
        carry = step(carry)
    _, right, left = lax.while_loop(busy, step, carry)
    me = where_ref[0]
    chip = me // 2
    sub = lax.broadcasted_iota(jnp.int32, (rows, LANES), 0)

    def row(array, index):
        return jnp.sum(jnp.where(sub == index, array, 0), axis=0, keepdims=True)

    core = me % 2
    arrived = jnp.where(core == 0, row(right[2], chip), row(left[2], chips - 1 - chip))
    behind = ((chip - origin) * (1 - 2 * core) > 0) & valid
    ends = jnp.full((1, LANES), -1, jnp.int32)
    for at, owner in enumerate((me, me + 1 - 2 * core)):
        for kind in range(2):
            hit = lane == kind * sectors + lists_ref[0, 2 * owner + kind]
            slot = jnp.where(behind, arrived, -1)
            if at == 0:
                slot = jnp.where(origin == chip, own_slot, slot)
            slot = jnp.sum(jnp.where(hit, slot + 1, 0), axis=1, keepdims=True) - 1
            ends = jnp.where(lane == 2 * at + kind, slot, ends)
    sends = jnp.where(core == 0, row(right[3] + 1, chip), row(left[3] + 1, chips - 1 - chip)) - 1
    table_ref[...] = jnp.concatenate([sends, ends, jnp.zeros((6, LANES), jnp.int32)], axis=0)
    count_ref[...] = jnp.broadcast_to(jnp.maximum(right[4], left[4]), (8, LANES))


def fetches(slot, stream, core, target, sem, blocks, pieces, tail):
    share = target.shape[0]
    half = pl.ds(stream * share, share)
    sources = []
    for at, block in enumerate(blocks):
        kind, other = at % 2, at // 2
        seat = core if other == 0 else 1 - core
        sources.append((slot == 2 * kind + seat, block.at[half]))
    for at, piece in enumerate(pieces):
        sources.append((slot == OWN + at, piece))
    if tail is not None:
        base = OWN + FIXED_ROUNDS
        sources.append((slot >= base, tail.at[jnp.clip(slot - base, 0, tail.shape[0] - 1)]))
    return [(use, pltpu.make_async_copy(source, target, sem)) for use, source in sources]


def run_copies(copies, verb):
    for use, copy in copies:

        @pl.when(use)
        def _(copy=copy):
            getattr(copy, verb)()


def stage_kernel(stream, has_tail, turn_ref, where_ref, table_ref, *refs):
    blocks, pieces, (out_ref, sem) = refs[:4], list(refs[4:-2]), refs[-2:]
    tail = pieces.pop() if has_tail else None
    slot = table_ref[0, turn_ref[0]]
    copies = fetches(slot, stream, where_ref[0] % 2, out_ref, sem.at[0], blocks, pieces, tail)
    run_copies(copies, "start")
    run_copies(copies, "wait")


def held_copies(kind, at, where_ref, table_ref, pieces, target, sems):
    blocks, pieces, tails = pieces[:4], pieces[4:-STREAMS], pieces[-STREAMS:]
    share = target.shape[0] // STREAMS
    copies = []
    for stream in range(STREAMS):
        copies += fetches(
            table_ref[1, 2 * at + kind],
            stream,
            where_ref[0] % 2,
            target.at[pl.ds(stream * share, share)],
            sems.at[kind * STREAMS + stream],
            blocks,
            pieces[stream * FIXED_ROUNDS : (stream + 1) * FIXED_ROUNDS],
            tails[stream],
        )
    return copies


def last_kernel(where_ref, table_ref, *refs):
    pieces, (out_ref, sems) = refs[:-2], refs[-2:]
    copies = []
    for kind in range(2):
        copies += held_copies(kind, 1, where_ref, table_ref, pieces, out_ref.at[kind], sems)
    run_copies(copies, "start")
    run_copies(copies, "wait")


def small_product(a, b):
    total = a[:, 0:1] * b[0:1, :]
    for k in range(1, 8):
        total = total + a[:, k : k + 1] * b[k : k + 1, :]
    return total


def finish_kernel(entries, me_ref, all_ref, basis_ref, state_ref, hess_ref):
    f32 = jnp.float32
    count = basis_ref.shape[0]
    sectors = all_ref.shape[0]
    data = all_ref[...]
    if sectors < LANES:
        data = jnp.concatenate([data, jnp.zeros((LANES - sectors, LANES), f32)], axis=0)
    data = data.T
    width = data.shape[1]
    sub = lax.broadcasted_iota(jnp.int32, (8, width), 0)
    lane = lax.broadcasted_iota(jnp.int32, (8, width), 1)
    start = data[7:8, :]
    moves = [data[8 * j : 8 * j + 8, :] for j in range(count)]
    moves[0] = jnp.where(sub == 7, 0.0, moves[0])
    grams = [data[64 + 8 * j : 64 + 8 * j + 8, :] for j in range(count)]

    def combine(columns, x, upto=count):
        total = columns[0] * x[0:1, :]
        for b in range(1, upto):
            total = total + columns[b] * x[b : b + 1, :]
        return total

    inner = [combine(grams, moves[j]) for j in range(count - 1)] + [moves[count - 1]]
    start_sq = jnp.sum(start * start * grams[0][0:1, :], axis=1, keepdims=True)
    basis = [jnp.where(sub == 0, start / jnp.sqrt(start_sq + EPS), 0.0)]
    hess = jnp.zeros((8, width), f32)
    for t in range(count):
        seen = combine(inner, basis[t], t + 1)
        stacked = jnp.zeros((8, width), f32)
        for s in range(t + 1):
            stacked = jnp.where(sub == s, jnp.sum(basis[s] * seen, axis=0, keepdims=True), stacked)
        h = jnp.sum(stacked, axis=1, keepdims=True)
        hess = jnp.where((lane == t) & (sub <= t), h, hess)
        if t + 1 < count:
            rest = combine(moves, basis[t], t + 1)
            for s in range(t + 1):
                rest = rest - h[s : s + 1, :] * basis[s]
            rest_sq = jnp.sum(rest * combine(grams, rest), keepdims=True)
            beta = jnp.sqrt(jnp.maximum(rest_sq, 0.0) + EPS)
            hess = jnp.where((lane == t) & (sub == t + 1), beta, hess)
            basis.append(rest / beta)
    hess_ref[...] = hess[:, :count]

    scaled = -TAU / 16.0 * hess
    term = jnp.where((sub == lane), 1.0, 0.0)
    series = term
    for order in range(1, 11):
        term = small_product(term, scaled) / float(order)
        series = series + term
    for square in range(4):
        series = small_product(series, series)
    coefficients = series[:, 0:1]
    norm = jnp.sum(coefficients * coefficients, axis=0, keepdims=True)
    rescale = jnp.sqrt(jnp.float32(entries)) / jnp.sqrt(norm)
    mine = jnp.zeros((8, width), f32)
    for t in range(count):
        mine = mine + coefficients[t : t + 1, :] * basis[t]
    mine = jnp.sum(jnp.where(lane == me_ref[0], mine, 0.0), axis=1, keepdims=True) * rescale
    step = 64
    for at in range(0, state_ref.shape[0], step):
        total = mine[0:1, :] * basis_ref[0, at : at + step, :]
        for i in range(1, count):
            total = total + mine[i : i + 1, :] * basis_ref[i, at : at + step, :]
        state_ref[at : at + step, :] = total


def shifted(x, step):
    group = lax.axis_size("group")
    return lax.ppermute(x, "group", [((k + step) % group, k) for k in range(group)])


def fetch_blocks(left_env, right_env, lists, mixing, sectors, me):
    channels, size = left_env.shape[0], left_env.shape[1]
    share = channels // STREAMS
    bf16 = left_env.dtype
    small = pl.BlockSpec(memory_space=pltpu.SMEM)
    whole = pl.BlockSpec(memory_space=pltpu.VMEM)
    place = pl.BlockSpec(memory_space=pl.ANY)
    swap = [(k, k + 1 - 2 * (k % 2)) for k in range(sectors)]
    along = [(k, k + 2) for k in range(0, sectors - 2, 2)]
    along += [(k, k - 2) for k in range(3, sectors, 2)]

    def pieces_of(*lead):
        return jax.ShapeDtypeStruct(lead + (share, size, size), bf16)

    where = me.reshape(1)
    blocks = [left_env, right_env] + [
        lax.ppermute(env, "sector", swap) for env in (left_env, right_env)
    ]
    table, count = pl.pallas_call(
        lambda *refs: route_kernel(sectors, *refs),
        out_shape=(jax.ShapeDtypeStruct((8, LANES), jnp.int32),) * 2,
        in_specs=[small, small],
        out_specs=(whole, whole),
        name="route",
    )(where, lists)
    rounds = spread_rows(count, "group", jnp.maximum, lax.pmax)[0, 0]

    def stage(stream, turn, held, tail=None):
        inputs = blocks + held + ([] if tail is None else [tail])
        return pl.pallas_call(
            lambda *refs: stage_kernel(stream, tail is not None, *refs),
            out_shape=pieces_of(),
            in_specs=[small] * 3 + [place] * len(inputs),
            out_specs=whole,
            scratch_shapes=[pltpu.SemaphoreType.DMA((1,))],
            name="stage",
        )(jnp.asarray(turn, jnp.int32).reshape(1), where, table, *inputs)

    held = [[] for _ in range(STREAMS)]
    for turn in range(FIXED_ROUNDS):
        for stream in range(STREAMS):
            flow = stage(stream, turn, held[stream])
            if (turn, stream) == (2, 0):
                flow, mixing = lax.optimization_barrier((flow, mixing))
            held[stream] = held[stream] + [lax.ppermute(flow, "sector", along)]

    def more(carry):
        return carry[0] < rounds

    def again(carry):
        turn, tails = carry
        moved = [
            lax.ppermute(stage(stream, turn, held[stream], tails[stream]), "sector", along)
            for stream in range(STREAMS)
        ]
        tails = [
            lax.dynamic_update_slice_in_dim(tail, piece[None], turn - FIXED_ROUNDS, axis=0)
            for tail, piece in zip(tails, moved)
        ]
        return turn + 1, tails

    room = pl.pallas_call(
        lambda *refs: None,
        out_shape=tuple(pieces_of(TAIL_ROUNDS) for _ in range(STREAMS)),
        out_specs=tuple(place for _ in range(STREAMS)),
        name="room",
    )()
    _, tails = lax.while_loop(more, again, (jnp.int32(FIXED_ROUNDS), list(room)))

    pieces = blocks + [piece for each in held for piece in each] + tails
    theirs = pl.pallas_call(
        last_kernel,
        out_shape=jax.ShapeDtypeStruct((2, channels, size, size), bf16),
        in_specs=[small] * 2 + [place] * len(pieces),
        out_specs=whole,
        scratch_shapes=[pltpu.SemaphoreType.DMA((2 * STREAMS,))],
        name="last",
    )(where, table, *pieces)
    return table, mixing, lax.ppermute(theirs, "sector", swap), pieces


def spread_blocks(left_env, right_env, lists, sectors):
    channels, size = left_env.shape[0], left_env.shape[1]
    sides = []
    for side, env in enumerate((left_env, right_env)):
        pieces = env.reshape(sectors, channels // sectors, size, size)
        spread = lax.all_to_all(pieces, "sector", split_axis=0, concat_axis=0, tiled=True)
        sends = jnp.take(spread, lists[0, side : 2 * sectors : 2], axis=0, mode="clip")
        sides.append(
            lax.all_to_all(sends, "sector", split_axis=0, concat_axis=0, tiled=True).reshape(
                channels, size, size
            )
        )
    return jnp.stack(sides)


def local(state, panel, left_env, right_env, left_match, right_match, phys_states):
    _, size, phys, _ = state.shape
    channels = left_env.shape[1]
    sector_count = lax.axis_size("sector")
    seat = lax.axis_index("sector").astype(jnp.int32)

    lane = lax.broadcasted_iota(jnp.int32, (8, LANES), 1)
    lists = jnp.where(lane == 2 * seat + 1, right_match, -1)
    lists = jnp.where(lane == 2 * seat, left_match, lists)
    lists = spread_rows(lists, "sector", jnp.maximum, lax.pmax)

    slices = [panel] + [shifted(panel, step) for step in range(1, lax.axis_size("group"))]
    mixing = arrange_mix(select_mix(slices, phys_states[0]), panel.shape[0])
    if sector_count <= 2 * LINE:
        table, mixing, theirs, pieces = fetch_blocks(
            left_env[0], right_env[0], lists, mixing, sector_count, seat
        )
    else:
        theirs, pieces = spread_blocks(left_env[0], right_env[0], lists, sector_count), []
        table = jnp.full((8, LANES), -1, jnp.int32)

    whole = pl.BlockSpec(memory_space=pltpu.VMEM)
    rows, f32, bf16 = size * phys, jnp.float32, jnp.bfloat16
    small = pl.BlockSpec(memory_space=pltpu.SMEM)
    place = pl.BlockSpec(memory_space=pl.ANY)
    devices = lax.axis_size("group") * sector_count
    me = (lax.axis_index("group").astype(jnp.int32) * sector_count + seat).reshape(1)
    basis, stats = pl.pallas_call(
        krylov_kernel,
        out_shape=(
            jax.ShapeDtypeStruct((KRYLOV, rows, size), f32),
            jax.ShapeDtypeStruct((devices, LANES), f32),
        ),
        in_specs=[small] * 2 + [whole] * 3 + [place] * len(pieces),
        out_specs=(whole, whole),
        scratch_shapes=[
            pltpu.VMEM((2, channels, size, size), bf16),
            pltpu.VMEM((channels * size, size), f32),
            pltpu.VMEM((channels * size, size), bf16),
            pltpu.VMEM((channels * size, size), bf16),
            pltpu.VMEM((size, rows), bf16),
            pltpu.VMEM((rows, channels * size), bf16),
            pltpu.VMEM((rows, size), f32),
            pltpu.SemaphoreType.DMA((2 * STREAMS,)),
        ],
        compiler_params=pltpu.CompilerParams(vmem_limit_bytes=40 * 1024 * 1024),
        name="krylov",
    )(table, me, state.reshape(rows, size), mixing, theirs, *pieces)

    gathered = spread_rows(stats, "sector", jnp.add, lax.psum)
    gathered = spread_rows(gathered, "group", jnp.add, lax.psum)
    entries = rows * size * devices
    evolved, hessenberg = pl.pallas_call(
        lambda *refs: finish_kernel(entries, *refs),
        out_shape=(
            jax.ShapeDtypeStruct((rows, size), f32),
            jax.ShapeDtypeStruct((KRYLOV, KRYLOV), f32),
        ),
        in_specs=[small, whole, whole],
        out_specs=(whole, whole),
        compiler_params=pltpu.CompilerParams(vmem_limit_bytes=24 * 1024 * 1024),
        name="finish",
    )(me, gathered, basis)
    return (evolved.reshape(state.shape), hessenberg)


def solution(mesh):
    return jax.shard_map(
        local,
        mesh=mesh,
        in_specs=(
            P(("group", "sector"), None, None, None),
            P("group", None, None),
            P(("group", "sector"), None, None, None),
            P(("group", "sector"), None, None, None),
            P(("group", "sector")),
            P(("group", "sector")),
            P(("group", "sector"), None),
        ),
        out_specs=(P(("group", "sector"), None, None, None), P()),
        check_vma=False,
    )
```

```python
import jax
import jax.numpy as jnp
from jax import lax
from jax.experimental import pallas as pl
from jax.experimental.pallas import tpu as pltpu
from jax.sharding import PartitionSpec as P

KRYLOV = 8
LOCAL = 16
TAU = 3.0
EPS = 1e-06
TINY = 1e-30
LANES = 128
STREAMS = 2
OWN = 4
FIXED_ROUNDS = 5
TAIL_ROUNDS = 7
SLOTS = 64
LINE = 4


def spread_rows(x, axis, combine, fallback):
    count = lax.axis_size(axis)
    if count & (count - 1):
        return fallback(x, axis)
    while count > 1:
        radix = 4 if count % 4 == 0 else 2
        count //= radix
        size = lax.axis_size(axis)
        others = [
            lax.ppermute(x, axis, [(k, k ^ (count * turn)) for k in range(size)])
            for turn in range(1, radix)
        ]
        for other in others:
            x = combine(x, other)
    return x


def select_mix(slices, states):
    pairs = states[:, None] * LOCAL + states[None, :]
    choose = (
        jnp.arange(slices[0].shape[2], dtype=jnp.int32)[None, None, :] == pairs[:, :, None]
    ).astype(jnp.bfloat16)
    panel = jnp.concatenate(slices, axis=0)
    mixed = jnp.einsum("acz,qpz->cpqa", panel, choose, preferred_element_type=jnp.float32)
    return mixed.astype(jnp.bfloat16)


def arrange_mix(mixed, share):
    group = lax.axis_size("group")
    turned = (group - lax.axis_index("group")) % group * share
    mixed = lax.dynamic_slice_in_dim(
        jnp.concatenate([mixed, mixed], axis=3), turned, mixed.shape[3], axis=3
    )
    channels, phys = mixed.shape[0], mixed.shape[1]
    same = jnp.eye(2, dtype=jnp.bfloat16)
    both = mixed[:, None, :, None] * same[None, :, None, :, None, None]
    return both.reshape(channels * 2 * phys, 2 * phys * channels)


def krylov_kernel(table_ref, me_ref, state_ref, mix_ref, theirs_ref, *refs):
    pieces, refs = refs[:-10], refs[-10:]
    basis_ref, stats_ref, mine_ref, wide_ref, rows_ref, turned_ref, x_ref, m_ref, w_ref, sems = refs
    channels, size = theirs_ref.shape[1], theirs_ref.shape[2]
    loads = []
    for kind in range(2):
        copies = []
        if pieces:
            copies = held_copies(kind, 0, me_ref, table_ref, pieces, mine_ref.at[kind], sems)
        received = pltpu.make_async_copy(
            theirs_ref.at[kind], mine_ref.at[kind], sems.at[2 * STREAMS + kind]
        )
        loads.append(copies + [(table_ref[1, kind] < 0, received)])
        run_copies(loads[kind], "start")
    phys = state_ref.shape[0] // size
    count = basis_ref.shape[0]
    f32, bf16 = jnp.float32, jnp.bfloat16

    basis_ref[...] = jnp.zeros_like(basis_ref)
    start = state_ref[...]
    start_sq = jnp.sum(start * start, keepdims=True)
    start_scale = jnp.sqrt(jnp.maximum(start_sq, TINY))
    basis_ref[0] = start / start_scale

    def load_left(part):
        def turn(n, carry):
            for k in range(8):
                wide_ref[pl.ds(8 * n + k, size, stride=channels), :] = part[0, 8 * n + k].astype(f32)
            return carry

        lax.fori_loop(0, channels // 8, turn, 0)

    def load_right(part):
        def turn(n, carry):
            for k in range(8):
                at = pl.multiple_of((8 * n + k) * size, size)
                turned_ref[pl.ds(at, size), :] = part[1, 8 * n + k].T
            return carry

        lax.fori_loop(0, channels // 8, turn, 0)

    for kind, load in enumerate((load_left, load_right)):
        run_copies(loads[kind], "wait")
        load(mine_ref)

    rows_ref[...] = wide_ref[...].astype(bf16)

    sub = lax.broadcasted_iota(jnp.int32, (8, LANES), 0)
    lane = lax.broadcasted_iota(jnp.int32, (8, LANES), 1)
    stats = jnp.where((sub == 7) & (lane == 7), start_scale, 0.0)

    group_rows = 4 * channels
    chunk = 64
    once = 64

    def column(j, stats):
        for q in range(phys):
            x_ref[:, q * size : (q + 1) * size] = basis_ref[
                j, pl.ds(q, size, stride=phys), :
            ].astype(bf16)

        def part(n, carry):
            for k in range(chunk // 4):
                if k % (once // 4) == 0:
                    at = n * chunk * channels + k * group_rows
                    at = pl.multiple_of(at, once * channels)
                    z = jnp.dot(
                        rows_ref[pl.ds(at, once * channels), :],
                        x_ref[...],
                        preferred_element_type=f32,
                    ).astype(bf16)
                first = k % (once // 4) * group_rows
                four = z[first : first + group_rows]
                halves = []
                for h in range(2):
                    pieces = []
                    for i2 in range(2):
                        base = (2 * h + i2) * channels
                        for q in range(phys):
                            pieces.append(
                                four[base : base + channels, q * size : (q + 1) * size]
                            )
                    halves.append(jnp.concatenate(pieces, axis=0))
                mixed = jnp.dot(
                    mix_ref[...], jnp.concatenate(halves, axis=1), preferred_element_type=f32
                )
                to = pl.multiple_of(n * chunk * phys, chunk * phys) + k * 4 * phys
                for c in range(channels):
                    block = mixed[c * 2 * phys : (c + 1) * 2 * phys]
                    m_ref[pl.ds(to, 4 * phys), c * size : (c + 1) * size] = jnp.concatenate(
                        [block[:, :size], block[:, size:]], axis=0
                    ).astype(bf16)
            return carry

        lax.fori_loop(0, size // chunk, part, 0)
        step = 64
        half = size * phys // 2
        sums = [jnp.zeros((8, LANES), f32) for _ in range(count + 1)]
        for start in range(0, size * phys, half):
            whole = jnp.dot(
                m_ref[start : start + half, :], turned_ref[...], preferred_element_type=f32
            )
            w_ref[start : start + half, :] = whole
            for at in range(start, start + half, step):
                w = whole[at - start : at - start + step]
                for i in range(count):
                    product = basis_ref[i, at : at + step, :] * w
                    sums[i] = sums[i] + jnp.sum(product.reshape(step // 8, 8, LANES), axis=0)
                sums[count] = sums[count] + jnp.sum((w * w).reshape(step // 8, 8, LANES), axis=0)
        stacked = jnp.zeros((8, LANES), f32)
        for i in range(count):
            stacked = jnp.where(sub == i, jnp.sum(sums[i], axis=0, keepdims=True), stacked)
        h = jnp.sum(stacked, axis=1, keepdims=True)
        w_sq = jnp.sum(sums[count], keepdims=True)
        left_sq = w_sq - jnp.sum(h * h, axis=0, keepdims=True)
        scale = jnp.sqrt(jnp.maximum(jnp.maximum(left_sq, 1e-10 * w_sq), TINY))
        inverse = 1.0 / scale

        @pl.when(j + 1 < count)
        def _():
            for at in range(0, size * phys, step):
                rest = w_ref[at : at + step, :]
                for i in range(count):
                    rest = rest - h[i : i + 1, :] * basis_ref[i, at : at + step, :]
                basis_ref[j + 1, at : at + step, :] = rest * inverse

        entry = jnp.where((sub == j + 1), scale, jnp.broadcast_to(h, (8, LANES)))
        return stats + jnp.where(lane == 8 * j + sub, entry, 0.0)

    stats = lax.fori_loop(0, count, column, stats)

    pairs = [(i, k) for i in range(count) for k in range(i + 1)]

    def gram(r, sums):
        for part in range(4):
            at = pl.multiple_of((4 * r + part) * 8, 8)
            rows = [basis_ref[i, pl.ds(at, 8), :] for i in range(count)]
            sums = [total + rows[i] * rows[k] for total, (i, k) in zip(sums, pairs)]
        return sums

    totals = lax.fori_loop(
        0, size * phys // 32, gram, [jnp.zeros((8, LANES), f32) for _ in pairs]
    )
    for first in range(0, len(pairs), 8):
        stacked = jnp.zeros((8, LANES), f32)
        place = jnp.full((8, LANES), -1, jnp.int32)
        mirror = place
        for row, (i, k) in enumerate(pairs[first : first + 8]):
            value = jnp.sum(totals[first + row], axis=0, keepdims=True)
            stacked = jnp.where(sub == row, value, stacked)
            place = jnp.where(sub == row, 64 + 8 * i + k, place)
            mirror = jnp.where(sub == row, 64 + 8 * k + i, mirror)
        value = jnp.sum(stacked, axis=1, keepdims=True)
        stats = stats + jnp.where((lane == place) | (lane == mirror), value, 0.0)
    seats = lax.broadcasted_iota(jnp.int32, stats_ref.shape, 0)
    stats_ref[...] = jnp.where(seats == me_ref[0], jnp.sum(stats, axis=0, keepdims=True), 0.0)


def schedule(origin, reach, own_slot, rows):
    sub = lax.broadcasted_iota(jnp.int32, (rows, LANES), 0)
    lane = lax.broadcasted_iota(jnp.int32, (rows, LANES), 1)
    wanted = (origin <= sub) & (reach > sub)
    score = jnp.where(wanted, (reach * LANES + lane) * SLOTS, -1)
    ready = jnp.where(wanted & (origin == sub), score + own_slot, -1)
    later = jnp.where(origin == sub, -1, score)

    def step(carry, turn):
        ready, later, held, table, used = carry
        best = jnp.max(ready, axis=1, keepdims=True)
        chosen = (ready == best) & (best >= 0)
        table = jnp.where(lane == turn, jnp.where(best >= 0, best & (SLOTS - 1), -1), table)
        used = jnp.where(jnp.max(best, axis=0, keepdims=True) >= 0, turn + 1, used)
        passed = jnp.where(chosen, 1, 0)
        arrived = jnp.concatenate([jnp.zeros((1, LANES), jnp.int32), passed[:-1]], axis=0) > 0
        slot = OWN + turn
        ready = jnp.where(chosen, -1, ready)
        ready = jnp.where(arrived & (later >= 0), later + slot, ready)
        later = jnp.where(arrived, -1, later)
        return ready, later, jnp.where(arrived, slot, held), table, used

    start = jnp.zeros((rows, LANES), jnp.int32)
    return (ready, later, start, start - 1, jnp.zeros((1, 1), jnp.int32)), step


def route_kernel(sectors, where_ref, lists_ref, table_ref, count_ref):
    chips = sectors // 2
    rows = -(-chips // 8) * 8
    lane = lax.broadcasted_iota(jnp.int32, (1, LANES), 1)
    valid = lane < 2 * sectors
    block = lane % sectors
    origin = jnp.where(valid, block // 2, chips)
    own_slot = 2 * (lane // sectors) + block % 2
    reach = jnp.full((1, LANES), -1, jnp.int32)
    back = jnp.full((1, LANES), -1, jnp.int32)
    for k in range(sectors):
        asked = jnp.where(lane < sectors, lists_ref[0, 2 * k], lists_ref[0, 2 * k + 1])
        hit = (block == asked) & valid
        reach = jnp.where(hit, k // 2, reach)
        back = jnp.where(hit, jnp.maximum(back, chips - 1 - k // 2), back)
    right, right_step = schedule(origin, reach, own_slot, rows)
    mirrored = jnp.where(valid, chips - 1 - origin, chips)
    left, left_step = schedule(mirrored, back, own_slot, rows)

    def busy(carry):
        _, right, left = carry
        return jnp.maximum(jnp.max(right[0]), jnp.max(left[0])) >= 0

    def step(carry):
        turn, right, left = carry
        return turn + 1, right_step(right, turn), left_step(left, turn)

    carry = (jnp.int32(0), right, left)
    for _ in range(FIXED_ROUNDS):
        carry = step(carry)
    _, right, left = lax.while_loop(busy, step, carry)
    me = where_ref[0]
    chip = me // 2
    sub = lax.broadcasted_iota(jnp.int32, (rows, LANES), 0)

    def row(array, index):
        return jnp.sum(jnp.where(sub == index, array, 0), axis=0, keepdims=True)

    core = me % 2
    arrived = jnp.where(core == 0, row(right[2], chip), row(left[2], chips - 1 - chip))
    behind = ((chip - origin) * (1 - 2 * core) > 0) & valid
    ends = jnp.full((1, LANES), -1, jnp.int32)
    for at, owner in enumerate((me, me + 1 - 2 * core)):
        for kind in range(2):
            hit = lane == kind * sectors + lists_ref[0, 2 * owner + kind]
            slot = jnp.where(behind, arrived, -1)
            if at == 0:
                slot = jnp.where(origin == chip, own_slot, slot)
            slot = jnp.sum(jnp.where(hit, slot + 1, 0), axis=1, keepdims=True) - 1
            ends = jnp.where(lane == 2 * at + kind, slot, ends)
    sends = jnp.where(core == 0, row(right[3] + 1, chip), row(left[3] + 1, chips - 1 - chip)) - 1
    table_ref[...] = jnp.concatenate([sends, ends, jnp.zeros((6, LANES), jnp.int32)], axis=0)
    count_ref[...] = jnp.broadcast_to(jnp.maximum(right[4], left[4]), (8, LANES))


def fetches(slot, stream, core, target, sem, blocks, pieces, tail):
    share = target.shape[0]
    half = pl.ds(stream * share, share)
    sources = []
    for at, block in enumerate(blocks):
        kind, other = at % 2, at // 2
        seat = core if other == 0 else 1 - core
        sources.append((slot == 2 * kind + seat, block.at[half]))
    for at, piece in enumerate(pieces):
        sources.append((slot == OWN + at, piece))
    if tail is not None:
        base = OWN + FIXED_ROUNDS
        sources.append((slot >= base, tail.at[jnp.clip(slot - base, 0, tail.shape[0] - 1)]))
    return [(use, pltpu.make_async_copy(source, target, sem)) for use, source in sources]


def run_copies(copies, verb):
    for use, copy in copies:

        @pl.when(use)
        def _(copy=copy):
            getattr(copy, verb)()


def stage_kernel(stream, has_tail, turn_ref, where_ref, table_ref, *refs):
    blocks, pieces, (out_ref, sem) = refs[:4], list(refs[4:-2]), refs[-2:]
    tail = pieces.pop() if has_tail else None
    slot = table_ref[0, turn_ref[0]]
    copies = fetches(slot, stream, where_ref[0] % 2, out_ref, sem.at[0], blocks, pieces, tail)
    run_copies(copies, "start")
    run_copies(copies, "wait")


def held_copies(kind, at, where_ref, table_ref, pieces, target, sems):
    blocks, pieces, tails = pieces[:4], pieces[4:-STREAMS], pieces[-STREAMS:]
    share = target.shape[0] // STREAMS
    copies = []
    for stream in range(STREAMS):
        copies += fetches(
            table_ref[1, 2 * at + kind],
            stream,
            where_ref[0] % 2,
            target.at[pl.ds(stream * share, share)],
            sems.at[kind * STREAMS + stream],
            blocks,
            pieces[stream * FIXED_ROUNDS : (stream + 1) * FIXED_ROUNDS],
            tails[stream],
        )
    return copies


def last_kernel(where_ref, table_ref, *refs):
    pieces, (out_ref, sems) = refs[:-2], refs[-2:]
    copies = []
    for kind in range(2):
        copies += held_copies(kind, 1, where_ref, table_ref, pieces, out_ref.at[kind], sems)
    run_copies(copies, "start")
    run_copies(copies, "wait")


def small_product(a, b):
    total = a[:, 0:1] * b[0:1, :]
    for k in range(1, 8):
        total = total + a[:, k : k + 1] * b[k : k + 1, :]
    return total


def finish_kernel(entries, me_ref, *refs):
    f32 = jnp.float32
    parts, (basis_ref, state_ref, hess_ref) = refs[:-3], refs[-3:]
    count = basis_ref.shape[0]
    sectors = parts[0].shape[0]
    data = parts[0][...]
    for part in parts[1:]:
        data = data + part[...]
    if sectors < LANES:
        data = jnp.concatenate([data, jnp.zeros((LANES - sectors, LANES), f32)], axis=0)
    data = data.T
    width = data.shape[1]
    sub = lax.broadcasted_iota(jnp.int32, (8, width), 0)
    lane = lax.broadcasted_iota(jnp.int32, (8, width), 1)
    start = data[7:8, :]
    moves = [data[8 * j : 8 * j + 8, :] for j in range(count)]
    moves[0] = jnp.where(sub == 7, 0.0, moves[0])
    grams = [data[64 + 8 * j : 64 + 8 * j + 8, :] for j in range(count)]

    def combine(columns, x, upto=count):
        total = columns[0] * x[0:1, :]
        for b in range(1, upto):
            total = total + columns[b] * x[b : b + 1, :]
        return total

    inner = [combine(grams, moves[j]) for j in range(count - 1)] + [moves[count - 1]]
    start_sq = jnp.sum(start * start * grams[0][0:1, :], axis=1, keepdims=True)
    basis = [jnp.where(sub == 0, start / jnp.sqrt(start_sq + EPS), 0.0)]
    hess = jnp.zeros((8, width), f32)
    for t in range(count):
        seen = combine(inner, basis[t], t + 1)
        stacked = jnp.zeros((8, width), f32)
        for s in range(t + 1):
            stacked = jnp.where(sub == s, jnp.sum(basis[s] * seen, axis=0, keepdims=True), stacked)
        h = jnp.sum(stacked, axis=1, keepdims=True)
        hess = jnp.where((lane == t) & (sub <= t), h, hess)
        if t + 1 < count:
            rest = combine(moves, basis[t], t + 1)
            for s in range(t + 1):
                rest = rest - h[s : s + 1, :] * basis[s]
            rest_sq = jnp.sum(rest * combine(grams, rest), keepdims=True)
            beta = jnp.sqrt(jnp.maximum(rest_sq, 0.0) + EPS)
            hess = jnp.where((lane == t) & (sub == t + 1), beta, hess)
            basis.append(rest / beta)
    hess_ref[...] = hess[:, :count]

    scaled = -TAU / 16.0 * hess
    term = jnp.where((sub == lane), 1.0, 0.0)
    series = term
    for order in range(1, 11):
        term = small_product(term, scaled) / float(order)
        series = series + term
    for square in range(4):
        series = small_product(series, series)
    coefficients = series[:, 0:1]
    norm = jnp.sum(coefficients * coefficients, axis=0, keepdims=True)
    rescale = jnp.sqrt(jnp.float32(entries)) / jnp.sqrt(norm)
    mine = jnp.zeros((8, width), f32)
    for t in range(count):
        mine = mine + coefficients[t : t + 1, :] * basis[t]
    mine = jnp.sum(jnp.where(lane == me_ref[0], mine, 0.0), axis=1, keepdims=True) * rescale
    step = 64
    for at in range(0, state_ref.shape[0], step):
        total = mine[0:1, :] * basis_ref[0, at : at + step, :]
        for i in range(1, count):
            total = total + mine[i : i + 1, :] * basis_ref[i, at : at + step, :]
        state_ref[at : at + step, :] = total


def shifted(x, step):
    group = lax.axis_size("group")
    return lax.ppermute(x, "group", [((k + step) % group, k) for k in range(group)])


def fetch_blocks(left_env, right_env, lists, mixing, sectors, me):
    channels, size = left_env.shape[0], left_env.shape[1]
    share = channels // STREAMS
    bf16 = left_env.dtype
    small = pl.BlockSpec(memory_space=pltpu.SMEM)
    whole = pl.BlockSpec(memory_space=pltpu.VMEM)
    place = pl.BlockSpec(memory_space=pl.ANY)
    swap = [(k, k + 1 - 2 * (k % 2)) for k in range(sectors)]
    along = [(k, k + 2) for k in range(0, sectors - 2, 2)]
    along += [(k, k - 2) for k in range(3, sectors, 2)]

    def pieces_of(*lead):
        return jax.ShapeDtypeStruct(lead + (share, size, size), bf16)

    where = me.reshape(1)
    blocks = [left_env, right_env] + [
        lax.ppermute(env, "sector", swap) for env in (left_env, right_env)
    ]
    table, count = pl.pallas_call(
        lambda *refs: route_kernel(sectors, *refs),
        out_shape=(jax.ShapeDtypeStruct((8, LANES), jnp.int32),) * 2,
        in_specs=[small, small],
        out_specs=(whole, whole),
        name="route",
    )(where, lists)
    rounds = spread_rows(count, "group", jnp.maximum, lax.pmax)[0, 0]

    def stage(stream, turn, held, tail=None):
        inputs = blocks + held + ([] if tail is None else [tail])
        return pl.pallas_call(
            lambda *refs: stage_kernel(stream, tail is not None, *refs),
            out_shape=pieces_of(),
            in_specs=[small] * 3 + [place] * len(inputs),
            out_specs=whole,
            scratch_shapes=[pltpu.SemaphoreType.DMA((1,))],
            name="stage",
        )(jnp.asarray(turn, jnp.int32).reshape(1), where, table, *inputs)

    held = [[] for _ in range(STREAMS)]
    for turn in range(FIXED_ROUNDS):
        for stream in range(STREAMS):
            flow = stage(stream, turn, held[stream])
            if (turn, stream) == (2, 0):
                flow, mixing = lax.optimization_barrier((flow, mixing))
            held[stream] = held[stream] + [lax.ppermute(flow, "sector", along)]

    def exchange(tails):
        pieces = blocks + [piece for each in held for piece in each] + tails
        theirs = pl.pallas_call(
            last_kernel,
            out_shape=jax.ShapeDtypeStruct((2, channels, size, size), bf16),
            in_specs=[small] * 2 + [place] * len(pieces),
            out_specs=whole,
            scratch_shapes=[pltpu.SemaphoreType.DMA((2 * STREAMS,))],
            name="last",
        )(where, table, *pieces)
        return lax.ppermute(theirs, "sector", swap)

    def more(carry):
        return carry[0] < rounds

    def again(carry):
        turn, tails, _ = carry
        moved = [
            lax.ppermute(stage(stream, turn, held[stream], tails[stream]), "sector", along)
            for stream in range(STREAMS)
        ]
        tails = [
            lax.dynamic_update_slice_in_dim(tail, piece[None], turn - FIXED_ROUNDS, axis=0)
            for tail, piece in zip(tails, moved)
        ]
        return turn + 1, tails, exchange(tails)

    room = pl.pallas_call(
        lambda *refs: None,
        out_shape=tuple(pieces_of(TAIL_ROUNDS) for _ in range(STREAMS)),
        out_specs=tuple(place for _ in range(STREAMS)),
        name="room",
    )()
    _, tails, theirs = lax.while_loop(
        more, again, (jnp.int32(FIXED_ROUNDS), list(room), exchange(list(room)))
    )
    pieces = blocks + [piece for each in held for piece in each] + tails
    return table, mixing, theirs, pieces


def spread_blocks(left_env, right_env, lists, sectors):
    channels, size = left_env.shape[0], left_env.shape[1]
    sides = []
    for side, env in enumerate((left_env, right_env)):
        pieces = env.reshape(sectors, channels // sectors, size, size)
        spread = lax.all_to_all(pieces, "sector", split_axis=0, concat_axis=0, tiled=True)
        sends = jnp.take(spread, lists[0, side : 2 * sectors : 2], axis=0, mode="clip")
        sides.append(
            lax.all_to_all(sends, "sector", split_axis=0, concat_axis=0, tiled=True).reshape(
                channels, size, size
            )
        )
    return jnp.stack(sides)


def local(state, panel, left_env, right_env, left_match, right_match, phys_states):
    _, size, phys, _ = state.shape
    channels = left_env.shape[1]
    sector_count = lax.axis_size("sector")
    seat = lax.axis_index("sector").astype(jnp.int32)

    lane = lax.broadcasted_iota(jnp.int32, (8, LANES), 1)
    lists = jnp.where(lane == 2 * seat + 1, right_match, -1)
    lists = jnp.where(lane == 2 * seat, left_match, lists)
    lists = spread_rows(lists, "sector", jnp.maximum, lax.pmax)

    slices = [panel] + [shifted(panel, step) for step in range(1, lax.axis_size("group"))]
    mixing = arrange_mix(select_mix(slices, phys_states[0]), panel.shape[0])
    if sector_count <= 2 * LINE:
        table, mixing, theirs, pieces = fetch_blocks(
            left_env[0], right_env[0], lists, mixing, sector_count, seat
        )
    else:
        theirs, pieces = spread_blocks(left_env[0], right_env[0], lists, sector_count), []
        table = jnp.full((8, LANES), -1, jnp.int32)

    whole = pl.BlockSpec(memory_space=pltpu.VMEM)
    rows, f32, bf16 = size * phys, jnp.float32, jnp.bfloat16
    small = pl.BlockSpec(memory_space=pltpu.SMEM)
    place = pl.BlockSpec(memory_space=pl.ANY)
    devices = lax.axis_size("group") * sector_count
    me = (lax.axis_index("group").astype(jnp.int32) * sector_count + seat).reshape(1)
    basis, stats = pl.pallas_call(
        krylov_kernel,
        out_shape=(
            jax.ShapeDtypeStruct((KRYLOV, rows, size), f32),
            jax.ShapeDtypeStruct((devices, LANES), f32),
        ),
        in_specs=[small] * 2 + [whole] * 2 + [place] * (1 + len(pieces)),
        out_specs=(whole, whole),
        scratch_shapes=[
            pltpu.VMEM((2, channels, size, size), bf16),
            pltpu.VMEM((channels * size, size), f32),
            pltpu.VMEM((channels * size, size), bf16),
            pltpu.VMEM((channels * size, size), bf16),
            pltpu.VMEM((size, rows), bf16),
            pltpu.VMEM((rows, channels * size), bf16),
            pltpu.VMEM((rows, size), f32),
            pltpu.SemaphoreType.DMA((2 * STREAMS + 2,)),
        ],
        compiler_params=pltpu.CompilerParams(vmem_limit_bytes=40 * 1024 * 1024),
        name="krylov",
    )(table, me, state.reshape(rows, size), mixing, theirs, *pieces)

    gathered = spread_rows(stats, "sector", jnp.add, lax.psum)
    gathered = [gathered] + [
        shifted(gathered, step) for step in range(1, lax.axis_size("group"))
    ]
    entries = rows * size * devices
    evolved, hessenberg = pl.pallas_call(
        lambda *refs: finish_kernel(entries, *refs),
        out_shape=(
            jax.ShapeDtypeStruct((rows, size), f32),
            jax.ShapeDtypeStruct((KRYLOV, KRYLOV), f32),
        ),
        in_specs=[small] + [whole] * (len(gathered) + 1),
        out_specs=(whole, whole),
        compiler_params=pltpu.CompilerParams(vmem_limit_bytes=24 * 1024 * 1024),
        name="finish",
    )(me, *gathered, basis)
    return (evolved.reshape(state.shape), hessenberg)


def solution(mesh):
    return jax.shard_map(
        local,
        mesh=mesh,
        in_specs=(
            P(("group", "sector"), None, None, None),
            P("group", None, None),
            P(("group", "sector"), None, None, None),
            P(("group", "sector"), None, None, None),
            P(("group", "sector")),
            P(("group", "sector")),
            P(("group", "sector"), None),
        ),
        out_specs=(P(("group", "sector"), None, None, None), P()),
        check_vma=False,
    )
```

```python
import jax
import jax.numpy as jnp
from jax import lax
from jax.experimental import pallas as pl
from jax.experimental.pallas import tpu as pltpu
from jax.sharding import PartitionSpec as P

KRYLOV = 8
LOCAL = 16
TAU = 3.0
EPS = 1e-06
TINY = 1e-30
LANES = 128
STREAMS = 2
OWN = 4
FIXED_ROUNDS = 5
TAIL_ROUNDS = 7
SLOTS = 64
LINE = 4


def spread_rows(x, axis, combine, fallback):
    count = lax.axis_size(axis)
    if count & (count - 1):
        return fallback(x, axis)
    while count > 1:
        radix = 4 if count % 4 == 0 else 2
        count //= radix
        size = lax.axis_size(axis)
        others = [
            lax.ppermute(x, axis, [(k, k ^ (count * turn)) for k in range(size)])
            for turn in range(1, radix)
        ]
        for other in others:
            x = combine(x, other)
    return x


def select_mix(slices, states):
    pairs = states[:, None] * LOCAL + states[None, :]
    choose = (
        jnp.arange(slices[0].shape[2], dtype=jnp.int32)[None, None, :] == pairs[:, :, None]
    ).astype(jnp.bfloat16)
    panel = jnp.concatenate(slices, axis=0)
    mixed = jnp.einsum("acz,qpz->cpqa", panel, choose, preferred_element_type=jnp.float32)
    count = mixed.shape[0] * mixed.shape[1]
    return mixed.astype(jnp.bfloat16).reshape(count, count)


def two_row_mix(mixed, turned, channels, phys):
    f32, bf16 = jnp.float32, jnp.bfloat16
    count = mixed.shape[0]
    row = lax.broadcasted_iota(jnp.int32, (count, count), 0)
    col = lax.broadcasted_iota(jnp.int32, (count, count), 1)
    same = (row & -channels) == (col & -channels)
    moved = ((row + turned) & (channels - 1)) == (col & (channels - 1))
    order = jnp.where(same & moved, 1.0, 0.0).astype(bf16)
    mixed = jnp.dot(mixed, order, preferred_element_type=f32).astype(bf16)
    row = lax.broadcasted_iota(jnp.int32, (2 * count, count), 0)
    col = lax.broadcasted_iota(jnp.int32, (2 * count, count), 1)
    base = ((row & (-2 * phys)) >> 1) + (row & (phys - 1))
    halves = []
    for i2 in range(2):
        here = (base == col) & ((row & phys) == i2 * phys)
        widen = jnp.where(here, 1.0, 0.0).astype(bf16)
        halves.append(jnp.dot(widen, mixed, preferred_element_type=f32).astype(bf16))
    return halves


def krylov_kernel(table_ref, me_ref, state_ref, mix_ref, theirs_ref, *refs):
    pieces, refs = refs[:-11], refs[-11:]
    basis_ref, stats_ref, both_ref, mine_ref, wide_ref, rows_ref, turned_ref, x_ref, m_ref, w_ref, sems = refs
    channels, size = theirs_ref.shape[1], theirs_ref.shape[2]
    loads = []
    if pieces:
        loads = [
            held_copies(kind, 0, me_ref, table_ref, pieces, mine_ref.at[kind], sems)
            for kind in range(2)
        ]
        for copies in loads:
            run_copies(copies, "start")
    phys = state_ref.shape[0] // size
    for at, half in enumerate(two_row_mix(mix_ref[...], me_ref[1], channels, phys)):
        both_ref[:, at * half.shape[1] : (at + 1) * half.shape[1]] = half
    count = basis_ref.shape[0]
    f32, bf16 = jnp.float32, jnp.bfloat16

    def load_left(part):
        def turn(n, carry):
            for k in range(8):
                wide_ref[pl.ds(8 * n + k, size, stride=channels), :] = part[0, 8 * n + k].astype(f32)
            return carry

        lax.fori_loop(0, channels // 8, turn, 0)

    def load_right(part):
        def turn(n, carry):
            for k in range(8):
                at = pl.multiple_of((8 * n + k) * size, size)
                turned_ref[pl.ds(at, size), :] = part[1, 8 * n + k].T
            return carry

        lax.fori_loop(0, channels // 8, turn, 0)

    for kind, load in enumerate((load_left, load_right)):
        here = table_ref[1, kind] >= 0
        if loads:
            run_copies(loads[kind], "wait")

        @pl.when(here)
        def _(load=load):
            load(mine_ref)

        @pl.when(jnp.logical_not(here))
        def _(load=load):
            load(theirs_ref)

    rows_ref[...] = wide_ref[...].astype(bf16)

    basis_ref[...] = jnp.zeros_like(basis_ref)
    start = state_ref[...]
    start_sq = jnp.sum(start * start, keepdims=True)
    start_scale = jnp.sqrt(jnp.maximum(start_sq, TINY))
    basis_ref[0] = start / start_scale

    sub = lax.broadcasted_iota(jnp.int32, (8, LANES), 0)
    lane = lax.broadcasted_iota(jnp.int32, (8, LANES), 1)
    stats = jnp.where((sub == 7) & (lane == 7), start_scale, 0.0)

    group_rows = 4 * channels
    chunk = 64
    once = 64

    def column(j, stats):
        for q in range(phys):
            x_ref[:, q * size : (q + 1) * size] = basis_ref[
                j, pl.ds(q, size, stride=phys), :
            ].astype(bf16)

        def part(n, carry):
            for k in range(chunk // 4):
                if k % (once // 4) == 0:
                    at = n * chunk * channels + k * group_rows
                    at = pl.multiple_of(at, once * channels)
                    z = jnp.dot(
                        rows_ref[pl.ds(at, once * channels), :],
                        x_ref[...],
                        preferred_element_type=f32,
                    ).astype(bf16)
                first = k % (once // 4) * group_rows
                four = z[first : first + group_rows]
                halves = []
                for h in range(2):
                    pieces = []
                    for i2 in range(2):
                        base = (2 * h + i2) * channels
                        for q in range(phys):
                            pieces.append(
                                four[base : base + channels, q * size : (q + 1) * size]
                            )
                    halves.append(jnp.concatenate(pieces, axis=0))
                mixed = jnp.dot(
                    both_ref[...], jnp.concatenate(halves, axis=1), preferred_element_type=f32
                )
                to = pl.multiple_of(n * chunk * phys, chunk * phys) + k * 4 * phys
                for c in range(channels):
                    block = mixed[c * 2 * phys : (c + 1) * 2 * phys]
                    m_ref[pl.ds(to, 4 * phys), c * size : (c + 1) * size] = jnp.concatenate(
                        [block[:, :size], block[:, size:]], axis=0
                    ).astype(bf16)
            return carry

        lax.fori_loop(0, size // chunk, part, 0)
        step = 64
        half = size * phys // 2
        sums = [jnp.zeros((8, LANES), f32) for _ in range(count + 1)]
        for start in range(0, size * phys, half):
            whole = jnp.dot(
                m_ref[start : start + half, :], turned_ref[...], preferred_element_type=f32
            )
            w_ref[start : start + half, :] = whole
            for at in range(start, start + half, step):
                w = whole[at - start : at - start + step]
                for i in range(count):
                    product = basis_ref[i, at : at + step, :] * w
                    sums[i] = sums[i] + jnp.sum(product.reshape(step // 8, 8, LANES), axis=0)
                sums[count] = sums[count] + jnp.sum((w * w).reshape(step // 8, 8, LANES), axis=0)
        stacked = jnp.zeros((8, LANES), f32)
        for i in range(count):
            stacked = jnp.where(sub == i, jnp.sum(sums[i], axis=0, keepdims=True), stacked)
        h = jnp.sum(stacked, axis=1, keepdims=True)
        w_sq = jnp.sum(sums[count], keepdims=True)
        left_sq = w_sq - jnp.sum(h * h, axis=0, keepdims=True)
        scale = jnp.sqrt(jnp.maximum(jnp.maximum(left_sq, 1e-10 * w_sq), TINY))
        inverse = 1.0 / scale

        @pl.when(j + 1 < count)
        def _():
            for at in range(0, size * phys, step):
                rest = w_ref[at : at + step, :]
                for i in range(count):
                    rest = rest - h[i : i + 1, :] * basis_ref[i, at : at + step, :]
                basis_ref[j + 1, at : at + step, :] = rest * inverse

        entry = jnp.where((sub == j + 1), scale, jnp.broadcast_to(h, (8, LANES)))
        return stats + jnp.where(lane == 8 * j + sub, entry, 0.0)

    stats = lax.fori_loop(0, count, column, stats)

    pairs = [(i, k) for i in range(count) for k in range(i + 1)]

    def gram(r, sums):
        for part in range(4):
            at = pl.multiple_of((4 * r + part) * 8, 8)
            rows = [basis_ref[i, pl.ds(at, 8), :] for i in range(count)]
            sums = [total + rows[i] * rows[k] for total, (i, k) in zip(sums, pairs)]
        return sums

    totals = lax.fori_loop(
        0, size * phys // 32, gram, [jnp.zeros((8, LANES), f32) for _ in pairs]
    )
    for (i, k), total in zip(pairs, totals):
        value = jnp.sum(total, keepdims=True)
        here = (lane == 64 + 8 * i + k) | (lane == 64 + 8 * k + i)
        stats = stats + jnp.where(here & (sub == 0), value, 0.0)
    seats = lax.broadcasted_iota(jnp.int32, stats_ref.shape, 0)
    stats_ref[...] = jnp.where(seats == me_ref[0], jnp.sum(stats, axis=0, keepdims=True), 0.0)


def schedule(origin, reach, own_slot, rows):
    sub = lax.broadcasted_iota(jnp.int32, (rows, LANES), 0)
    lane = lax.broadcasted_iota(jnp.int32, (rows, LANES), 1)
    wanted = (origin <= sub) & (reach > sub)
    score = jnp.where(wanted, (reach * LANES + lane) * SLOTS, -1)
    ready = jnp.where(wanted & (origin == sub), score + own_slot, -1)
    later = jnp.where(origin == sub, -1, score)

    def step(carry, turn):
        ready, later, held, table, used = carry
        best = jnp.max(ready, axis=1, keepdims=True)
        chosen = (ready == best) & (best >= 0)
        table = jnp.where(lane == turn, jnp.where(best >= 0, best & (SLOTS - 1), -1), table)
        used = jnp.where(jnp.max(best, axis=0, keepdims=True) >= 0, turn + 1, used)
        passed = jnp.where(chosen, 1, 0)
        arrived = jnp.concatenate([jnp.zeros((1, LANES), jnp.int32), passed[:-1]], axis=0) > 0
        slot = OWN + turn
        ready = jnp.where(chosen, -1, ready)
        ready = jnp.where(arrived & (later >= 0), later + slot, ready)
        later = jnp.where(arrived, -1, later)
        return ready, later, jnp.where(arrived, slot, held), table, used

    start = jnp.zeros((rows, LANES), jnp.int32)
    return (ready, later, start, start - 1, jnp.zeros((1, 1), jnp.int32)), step


def route_kernel(sectors, where_ref, lists_ref, table_ref, count_ref):
    chips = sectors // 2
    rows = -(-chips // 8) * 8
    lane = lax.broadcasted_iota(jnp.int32, (1, LANES), 1)
    valid = lane < 2 * sectors
    block = lane % sectors
    origin = jnp.where(valid, block // 2, chips)
    own_slot = 2 * (lane // sectors) + block % 2
    reach = jnp.full((1, LANES), -1, jnp.int32)
    back = jnp.full((1, LANES), -1, jnp.int32)
    for k in range(sectors):
        asked = jnp.where(lane < sectors, lists_ref[0, 2 * k], lists_ref[0, 2 * k + 1])
        hit = (block == asked) & valid
        reach = jnp.where(hit, k // 2, reach)
        back = jnp.where(hit, jnp.maximum(back, chips - 1 - k // 2), back)
    right, right_step = schedule(origin, reach, own_slot, rows)
    mirrored = jnp.where(valid, chips - 1 - origin, chips)
    left, left_step = schedule(mirrored, back, own_slot, rows)

    def busy(carry):
        _, right, left = carry
        return jnp.maximum(jnp.max(right[0]), jnp.max(left[0])) >= 0

    def step(carry):
        turn, right, left = carry
        return turn + 1, right_step(right, turn), left_step(left, turn)

    carry = (jnp.int32(0), right, left)
    for _ in range(FIXED_ROUNDS):
        carry = step(carry)
    _, right, left = lax.while_loop(busy, step, carry)
    me = where_ref[0]
    chip = me // 2
    sub = lax.broadcasted_iota(jnp.int32, (rows, LANES), 0)

    def row(array, index):
        return jnp.sum(jnp.where(sub == index, array, 0), axis=0, keepdims=True)

    core = me % 2
    arrived = jnp.where(core == 0, row(right[2], chip), row(left[2], chips - 1 - chip))
    behind = ((chip - origin) * (1 - 2 * core) > 0) & valid
    ends = jnp.full((1, LANES), -1, jnp.int32)
    for at, owner in enumerate((me, me + 1 - 2 * core)):
        for kind in range(2):
            hit = lane == kind * sectors + lists_ref[0, 2 * owner + kind]
            slot = jnp.where(behind, arrived, -1)
            if at == 0:
                slot = jnp.where(origin == chip, own_slot, slot)
            slot = jnp.sum(jnp.where(hit, slot + 1, 0), axis=1, keepdims=True) - 1
            ends = jnp.where(lane == 2 * at + kind, slot, ends)
    sends = jnp.where(core == 0, row(right[3] + 1, chip), row(left[3] + 1, chips - 1 - chip)) - 1
    table_ref[...] = jnp.concatenate([sends, ends, jnp.zeros((6, LANES), jnp.int32)], axis=0)
    count_ref[...] = jnp.broadcast_to(jnp.maximum(right[4], left[4]), (8, LANES))


def fetches(slot, stream, core, target, sem, blocks, pieces, tail):
    share = target.shape[0]
    half = pl.ds(stream * share, share)
    sources = []
    for at, block in enumerate(blocks):
        kind, other = at % 2, at // 2
        seat = core if other == 0 else 1 - core
        sources.append((slot == 2 * kind + seat, block.at[half]))
    for at, piece in enumerate(pieces):
        sources.append((slot == OWN + at, piece))
    if tail is not None:
        base = OWN + FIXED_ROUNDS
        sources.append((slot >= base, tail.at[jnp.clip(slot - base, 0, tail.shape[0] - 1)]))
    return [(use, pltpu.make_async_copy(source, target, sem)) for use, source in sources]


def run_copies(copies, verb):
    for use, copy in copies:

        @pl.when(use)
        def _(copy=copy):
            getattr(copy, verb)()


def stage_kernel(stream, has_tail, turn_ref, where_ref, table_ref, *refs):
    blocks, pieces, (out_ref, sem) = refs[:4], list(refs[4:-2]), refs[-2:]
    tail = pieces.pop() if has_tail else None
    slot = table_ref[0, turn_ref[0]]
    copies = fetches(slot, stream, where_ref[0] % 2, out_ref, sem.at[0], blocks, pieces, tail)
    run_copies(copies, "start")
    run_copies(copies, "wait")


def held_copies(kind, at, where_ref, table_ref, pieces, target, sems):
    blocks, pieces, tails = pieces[:4], pieces[4:-STREAMS], pieces[-STREAMS:]
    share = target.shape[0] // STREAMS
    copies = []
    for stream in range(STREAMS):
        copies += fetches(
            table_ref[1, 2 * at + kind],
            stream,
            where_ref[0] % 2,
            target.at[pl.ds(stream * share, share)],
            sems.at[kind * STREAMS + stream],
            blocks,
            pieces[stream * FIXED_ROUNDS : (stream + 1) * FIXED_ROUNDS],
            tails[stream],
        )
    return copies


def last_kernel(where_ref, table_ref, *refs):
    pieces, (out_ref, sems) = refs[:-2], refs[-2:]
    copies = []
    for kind in range(2):
        copies += held_copies(kind, 1, where_ref, table_ref, pieces, out_ref.at[kind], sems)
    run_copies(copies, "start")
    run_copies(copies, "wait")


def small_product(a, b):
    total = a[:, 0:1] * b[0:1, :]
    for k in range(1, 8):
        total = total + a[:, k : k + 1] * b[k : k + 1, :]
    return total


def finish_kernel(entries, me_ref, all_ref, basis_ref, state_ref, hess_ref):
    f32 = jnp.float32
    count = basis_ref.shape[0]
    sectors = all_ref.shape[0]
    data = all_ref[...]
    if sectors < LANES:
        data = jnp.concatenate([data, jnp.zeros((LANES - sectors, LANES), f32)], axis=0)
    data = data.T
    width = data.shape[1]
    sub = lax.broadcasted_iota(jnp.int32, (8, width), 0)
    lane = lax.broadcasted_iota(jnp.int32, (8, width), 1)
    start = data[7:8, :]
    moves = [data[8 * j : 8 * j + 8, :] for j in range(count)]
    moves[0] = jnp.where(sub == 7, 0.0, moves[0])
    grams = [data[64 + 8 * j : 64 + 8 * j + 8, :] for j in range(count)]

    def combine(columns, x, upto=count):
        total = columns[0] * x[0:1, :]
        for b in range(1, upto):
            total = total + columns[b] * x[b : b + 1, :]
        return total

    inner = [combine(grams, moves[j]) for j in range(count - 1)] + [moves[count - 1]]
    start_sq = jnp.sum(start * start * grams[0][0:1, :], axis=1, keepdims=True)
    basis = [jnp.where(sub == 0, start / jnp.sqrt(start_sq + EPS), 0.0)]
    hess = jnp.zeros((8, width), f32)
    for t in range(count):
        seen = combine(inner, basis[t], t + 1)
        stacked = jnp.zeros((8, width), f32)
        for s in range(t + 1):
            stacked = jnp.where(sub == s, jnp.sum(basis[s] * seen, axis=0, keepdims=True), stacked)
        h = jnp.sum(stacked, axis=1, keepdims=True)
        hess = jnp.where((lane == t) & (sub <= t), h, hess)
        if t + 1 < count:
            rest = combine(moves, basis[t], t + 1)
            for s in range(t + 1):
                rest = rest - h[s : s + 1, :] * basis[s]
            rest_sq = jnp.sum(rest * combine(grams, rest), keepdims=True)
            beta = jnp.sqrt(jnp.maximum(rest_sq, 0.0) + EPS)
            hess = jnp.where((lane == t) & (sub == t + 1), beta, hess)
            basis.append(rest / beta)
    hess_ref[...] = hess[:, :count]

    scaled = -TAU / 16.0 * hess
    term = jnp.where((sub == lane), 1.0, 0.0)
    series = term
    for order in range(1, 11):
        term = small_product(term, scaled) / float(order)
        series = series + term
    for square in range(4):
        series = small_product(series, series)
    coefficients = series[:, 0:1]
    norm = jnp.sum(coefficients * coefficients, axis=0, keepdims=True)
    rescale = jnp.sqrt(jnp.float32(entries)) / jnp.sqrt(norm)
    mine = jnp.zeros((8, width), f32)
    for t in range(count):
        mine = mine + coefficients[t : t + 1, :] * basis[t]
    mine = jnp.sum(jnp.where(lane == me_ref[0], mine, 0.0), axis=1, keepdims=True) * rescale
    step = 64
    for at in range(0, state_ref.shape[0], step):
        total = mine[0:1, :] * basis_ref[0, at : at + step, :]
        for i in range(1, count):
            total = total + mine[i : i + 1, :] * basis_ref[i, at : at + step, :]
        state_ref[at : at + step, :] = total


def shifted(x, step):
    group = lax.axis_size("group")
    return lax.ppermute(x, "group", [((k + step) % group, k) for k in range(group)])


def fetch_blocks(left_env, right_env, lists, slices, sectors, me):
    channels, size = left_env.shape[0], left_env.shape[1]
    share = channels // STREAMS
    bf16 = left_env.dtype
    small = pl.BlockSpec(memory_space=pltpu.SMEM)
    whole = pl.BlockSpec(memory_space=pltpu.VMEM)
    place = pl.BlockSpec(memory_space=pl.ANY)
    swap = [(k, k + 1 - 2 * (k % 2)) for k in range(sectors)]
    along = [(k, k + 2) for k in range(0, sectors - 2, 2)]
    along += [(k, k - 2) for k in range(3, sectors, 2)]

    def pieces_of(*lead):
        return jax.ShapeDtypeStruct(lead + (share, size, size), bf16)

    where = me.reshape(1)
    blocks = [left_env, right_env] + [
        lax.ppermute(env, "sector", swap) for env in (left_env, right_env)
    ]
    table, count = pl.pallas_call(
        lambda *refs: route_kernel(sectors, *refs),
        out_shape=(jax.ShapeDtypeStruct((8, LANES), jnp.int32),) * 2,
        in_specs=[small, small],
        out_specs=(whole, whole),
        name="route",
    )(where, lists)
    rounds = spread_rows(count, "group", jnp.maximum, lax.pmax)[0, 0]

    def stage(stream, turn, held, tail=None):
        inputs = blocks + held + ([] if tail is None else [tail])
        return pl.pallas_call(
            lambda *refs: stage_kernel(stream, tail is not None, *refs),
            out_shape=pieces_of(),
            in_specs=[small] * 3 + [place] * len(inputs),
            out_specs=whole,
            scratch_shapes=[pltpu.SemaphoreType.DMA((1,))],
            name="stage",
        )(jnp.asarray(turn, jnp.int32).reshape(1), where, table, *inputs)

    held = [[] for _ in range(STREAMS)]
    for turn in range(FIXED_ROUNDS):
        for stream in range(STREAMS):
            flow = stage(stream, turn, held[stream])
            if (turn, stream) == (2, 0):
                flow, slices = lax.optimization_barrier((flow, slices))
            held[stream] = held[stream] + [lax.ppermute(flow, "sector", along)]

    def more(carry):
        return carry[0] < rounds

    def again(carry):
        turn, tails = carry
        moved = [
            lax.ppermute(stage(stream, turn, held[stream], tails[stream]), "sector", along)
            for stream in range(STREAMS)
        ]
        tails = [
            lax.dynamic_update_slice_in_dim(tail, piece[None], turn - FIXED_ROUNDS, axis=0)
            for tail, piece in zip(tails, moved)
        ]
        return turn + 1, tails

    room = pl.pallas_call(
        lambda *refs: None,
        out_shape=tuple(pieces_of(TAIL_ROUNDS) for _ in range(STREAMS)),
        out_specs=tuple(place for _ in range(STREAMS)),
        name="room",
    )()
    _, tails = lax.while_loop(more, again, (jnp.int32(FIXED_ROUNDS), list(room)))

    pieces = blocks + [piece for each in held for piece in each] + tails
    theirs = pl.pallas_call(
        last_kernel,
        out_shape=jax.ShapeDtypeStruct((2, channels, size, size), bf16),
        in_specs=[small] * 2 + [place] * len(pieces),
        out_specs=whole,
        scratch_shapes=[pltpu.SemaphoreType.DMA((2 * STREAMS,))],
        name="last",
    )(where, table, *pieces)
    theirs, slices = lax.optimization_barrier((theirs, slices))
    return table, slices, lax.ppermute(theirs, "sector", swap), pieces


def spread_blocks(left_env, right_env, lists, sectors):
    channels, size = left_env.shape[0], left_env.shape[1]
    sides = []
    for side, env in enumerate((left_env, right_env)):
        pieces = env.reshape(sectors, channels // sectors, size, size)
        spread = lax.all_to_all(pieces, "sector", split_axis=0, concat_axis=0, tiled=True)
        sends = jnp.take(spread, lists[0, side : 2 * sectors : 2], axis=0, mode="clip")
        sides.append(
            lax.all_to_all(sends, "sector", split_axis=0, concat_axis=0, tiled=True).reshape(
                channels, size, size
            )
        )
    return jnp.stack(sides)


def local(state, panel, left_env, right_env, left_match, right_match, phys_states):
    _, size, phys, _ = state.shape
    channels = left_env.shape[1]
    sector_count = lax.axis_size("sector")
    seat = lax.axis_index("sector").astype(jnp.int32)

    lane = lax.broadcasted_iota(jnp.int32, (8, LANES), 1)
    lists = jnp.where(lane == 2 * seat + 1, right_match, -1)
    lists = jnp.where(lane == 2 * seat, left_match, lists)
    lists = spread_rows(lists, "sector", jnp.maximum, lax.pmax)

    slices = [panel] + [shifted(panel, step) for step in range(1, lax.axis_size("group"))]
    if sector_count <= 2 * LINE:
        table, slices, theirs, pieces = fetch_blocks(
            left_env[0], right_env[0], lists, slices, sector_count, seat
        )
    else:
        theirs, pieces = spread_blocks(left_env[0], right_env[0], lists, sector_count), []
        table = jnp.full((8, LANES), -1, jnp.int32)
    mixing = select_mix(slices, phys_states[0])

    whole = pl.BlockSpec(memory_space=pltpu.VMEM)
    rows, f32, bf16 = size * phys, jnp.float32, jnp.bfloat16
    small = pl.BlockSpec(memory_space=pltpu.SMEM)
    place = pl.BlockSpec(memory_space=pl.ANY)
    devices = lax.axis_size("group") * sector_count
    group = lax.axis_index("group").astype(jnp.int32)
    me = jnp.stack([group * sector_count + seat, group * panel.shape[0]])
    basis, stats = pl.pallas_call(
        krylov_kernel,
        out_shape=(
            jax.ShapeDtypeStruct((KRYLOV, rows, size), f32),
            jax.ShapeDtypeStruct((devices, LANES), f32),
        ),
        in_specs=[small] * 2 + [whole] * 3 + [place] * len(pieces),
        out_specs=(whole, whole),
        scratch_shapes=[
            pltpu.VMEM((2 * phys * channels, 2 * phys * channels), bf16),
            pltpu.VMEM((2, channels, size, size), bf16),
            pltpu.VMEM((channels * size, size), f32),
            pltpu.VMEM((channels * size, size), bf16),
            pltpu.VMEM((channels * size, size), bf16),
            pltpu.VMEM((size, rows), bf16),
            pltpu.VMEM((rows, channels * size), bf16),
            pltpu.VMEM((rows, size), f32),
            pltpu.SemaphoreType.DMA((2 * STREAMS,)),
        ],
        compiler_params=pltpu.CompilerParams(vmem_limit_bytes=40 * 1024 * 1024),
        name="krylov",
    )(table, me, state.reshape(rows, size), mixing, theirs, *pieces)

    gathered = spread_rows(stats, "sector", jnp.add, lax.psum)
    gathered = spread_rows(gathered, "group", jnp.add, lax.psum)
    entries = rows * size * devices
    evolved, hessenberg = pl.pallas_call(
        lambda *refs: finish_kernel(entries, *refs),
        out_shape=(
            jax.ShapeDtypeStruct((rows, size), f32),
            jax.ShapeDtypeStruct((KRYLOV, KRYLOV), f32),
        ),
        in_specs=[small, whole, whole],
        out_specs=(whole, whole),
        compiler_params=pltpu.CompilerParams(vmem_limit_bytes=24 * 1024 * 1024),
        name="finish",
    )(me, gathered, basis)
    return (evolved.reshape(state.shape), hessenberg)


def solution(mesh):
    return jax.shard_map(
        local,
        mesh=mesh,
        in_specs=(
            P(("group", "sector"), None, None, None),
            P("group", None, None),
            P(("group", "sector"), None, None, None),
            P(("group", "sector"), None, None, None),
            P(("group", "sector")),
            P(("group", "sector")),
            P(("group", "sector"), None),
        ),
        out_specs=(P(("group", "sector"), None, None, None), P()),
        check_vma=False,
    )
```

```python
import jax
import jax.numpy as jnp
from jax import lax
from jax.experimental import pallas as pl
from jax.experimental.pallas import tpu as pltpu
from jax.sharding import PartitionSpec as P

KRYLOV = 8
LOCAL = 16
TAU = 3.0
EPS = 1e-06
TINY = 1e-30
LANES = 128
STREAMS = 2
OWN = 4
FIXED_ROUNDS = 5
TAIL_ROUNDS = 7
SLOTS = 64
LINE = 4


def spread_rows(x, axis, combine, fallback):
    count = lax.axis_size(axis)
    if count & (count - 1):
        return fallback(x, axis)
    while count > 1:
        radix = 4 if count % 4 == 0 else 2
        count //= radix
        size = lax.axis_size(axis)
        others = [
            lax.ppermute(x, axis, [(k, k ^ (count * turn)) for k in range(size)])
            for turn in range(1, radix)
        ]
        for other in others:
            x = combine(x, other)
    return x


def select_mix(slices, states):
    pairs = states[:, None] * LOCAL + states[None, :]
    choose = (
        jnp.arange(slices[0].shape[2], dtype=jnp.int32)[None, None, :] == pairs[:, :, None]
    ).astype(jnp.bfloat16)
    panel = jnp.concatenate(slices, axis=0)
    mixed = jnp.einsum("acz,qpz->cpqa", panel, choose, preferred_element_type=jnp.float32)
    return mixed.astype(jnp.bfloat16)


def arrange_mix(mixed, share):
    group = lax.axis_size("group")
    turned = (group - lax.axis_index("group")) % group * share
    mixed = lax.dynamic_slice_in_dim(
        jnp.concatenate([mixed, mixed], axis=3), turned, mixed.shape[3], axis=3
    )
    channels, phys = mixed.shape[0], mixed.shape[1]
    same = jnp.eye(2, dtype=jnp.bfloat16)
    both = mixed[:, None, :, None] * same[None, :, None, :, None, None]
    return both.reshape(channels * 2 * phys, 2 * phys * channels)


def krylov_kernel(table_ref, me_ref, state_ref, mix_ref, theirs_ref, *refs):
    pieces, refs = refs[:-10], refs[-10:]
    basis_ref, stats_ref, mine_ref, wide_ref, rows_ref, turned_ref, x_ref, m_ref, w_ref, sems = refs
    channels, size = theirs_ref.shape[1], theirs_ref.shape[2]
    loads = []
    if pieces:
        loads = [
            held_copies(kind, 0, me_ref, table_ref, pieces, mine_ref.at[kind], sems)
            for kind in range(2)
        ]
        for copies in loads:
            run_copies(copies, "start")
    phys = state_ref.shape[0] // size
    count = basis_ref.shape[0]
    f32, bf16 = jnp.float32, jnp.bfloat16

    def load_left(part):
        def turn(n, carry):
            for k in range(8):
                wide_ref[pl.ds(8 * n + k, size, stride=channels), :] = part[0, 8 * n + k].astype(f32)
            return carry

        lax.fori_loop(0, channels // 8, turn, 0)

    def load_right(part):
        def turn(n, carry):
            for k in range(8):
                at = pl.multiple_of((8 * n + k) * size, size)
                turned_ref[pl.ds(at, size), :] = part[1, 8 * n + k].T
            return carry

        lax.fori_loop(0, channels // 8, turn, 0)

    for kind, load in enumerate((load_left, load_right)):
        here = table_ref[1, kind] >= 0
        if loads:
            run_copies(loads[kind], "wait")

        @pl.when(here)
        def _(load=load):
            load(mine_ref)

        @pl.when(jnp.logical_not(here))
        def _(load=load):
            load(theirs_ref)

    rows_ref[...] = wide_ref[...].astype(bf16)

    basis_ref[...] = jnp.zeros_like(basis_ref)
    start = state_ref[...]
    start_sq = jnp.sum(start * start, keepdims=True)
    start_scale = jnp.sqrt(jnp.maximum(start_sq, TINY))
    basis_ref[0] = start / start_scale

    sub = lax.broadcasted_iota(jnp.int32, (8, LANES), 0)
    lane = lax.broadcasted_iota(jnp.int32, (8, LANES), 1)
    stats = jnp.where((sub == 7) & (lane == 7), start_scale, 0.0)

    group_rows = 4 * channels
    chunk = 64
    once = 32

    def column(j, stats):
        for q in range(phys):
            x_ref[:, q * size : (q + 1) * size] = basis_ref[
                j, pl.ds(q, size, stride=phys), :
            ].astype(bf16)

        def part(n, carry):
            for k in range(chunk // 4):
                if k % (once // 4) == 0:
                    at = n * chunk * channels + k * group_rows
                    at = pl.multiple_of(at, once * channels)
                    z = jnp.dot(
                        rows_ref[pl.ds(at, once * channels), :],
                        x_ref[...],
                        preferred_element_type=f32,
                    ).astype(bf16)
                first = k % (once // 4) * group_rows
                four = z[first : first + group_rows]
                halves = []
                for h in range(2):
                    pieces = []
                    for i2 in range(2):
                        base = (2 * h + i2) * channels
                        for q in range(phys):
                            pieces.append(
                                four[base : base + channels, q * size : (q + 1) * size]
                            )
                    halves.append(jnp.concatenate(pieces, axis=0))
                mixed = jnp.dot(
                    mix_ref[...], jnp.concatenate(halves, axis=1), preferred_element_type=f32
                )
                to = pl.multiple_of(n * chunk * phys, chunk * phys) + k * 4 * phys
                for c in range(channels):
                    block = mixed[c * 2 * phys : (c + 1) * 2 * phys]
                    m_ref[pl.ds(to, 4 * phys), c * size : (c + 1) * size] = jnp.concatenate(
                        [block[:, :size], block[:, size:]], axis=0
                    ).astype(bf16)
            return carry

        lax.fori_loop(0, size // chunk, part, 0)
        step = 64
        half = size * phys // 2
        sums = [jnp.zeros((8, LANES), f32) for _ in range(count + 1)]
        for start in range(0, size * phys, half):
            whole = jnp.dot(
                m_ref[start : start + half, :], turned_ref[...], preferred_element_type=f32
            )
            w_ref[start : start + half, :] = whole
            for at in range(start, start + half, step):
                w = whole[at - start : at - start + step]
                for i in range(count):
                    product = basis_ref[i, at : at + step, :] * w
                    sums[i] = sums[i] + jnp.sum(product.reshape(step // 8, 8, LANES), axis=0)
                sums[count] = sums[count] + jnp.sum((w * w).reshape(step // 8, 8, LANES), axis=0)
        stacked = jnp.zeros((8, LANES), f32)
        for i in range(count):
            stacked = jnp.where(sub == i, jnp.sum(sums[i], axis=0, keepdims=True), stacked)
        h = jnp.sum(stacked, axis=1, keepdims=True)
        w_sq = jnp.sum(sums[count], keepdims=True)
        left_sq = w_sq - jnp.sum(h * h, axis=0, keepdims=True)
        scale = jnp.sqrt(jnp.maximum(jnp.maximum(left_sq, 1e-10 * w_sq), TINY))
        inverse = 1.0 / scale

        @pl.when(j + 1 < count)
        def _():
            for at in range(0, size * phys, step):
                rest = w_ref[at : at + step, :]
                for i in range(count):
                    rest = rest - h[i : i + 1, :] * basis_ref[i, at : at + step, :]
                basis_ref[j + 1, at : at + step, :] = rest * inverse

        entry = jnp.where((sub == j + 1), scale, jnp.broadcast_to(h, (8, LANES)))
        return stats + jnp.where(lane == 8 * j + sub, entry, 0.0)

    stats = lax.fori_loop(0, count, column, stats)

    pairs = [(i, k) for i in range(count) for k in range(i + 1)]

    def gram(r, sums):
        for part in range(4):
            at = pl.multiple_of((4 * r + part) * 8, 8)
            rows = [basis_ref[i, pl.ds(at, 8), :] for i in range(count)]
            sums = [total + rows[i] * rows[k] for total, (i, k) in zip(sums, pairs)]
        return sums

    totals = lax.fori_loop(
        0, size * phys // 32, gram, [jnp.zeros((8, LANES), f32) for _ in pairs]
    )
    for (i, k), total in zip(pairs, totals):
        value = jnp.sum(total, keepdims=True)
        here = (lane == 64 + 8 * i + k) | (lane == 64 + 8 * k + i)
        stats = stats + jnp.where(here & (sub == 0), value, 0.0)
    seats = lax.broadcasted_iota(jnp.int32, stats_ref.shape, 0)
    stats_ref[...] = jnp.where(seats == me_ref[0], jnp.sum(stats, axis=0, keepdims=True), 0.0)


def schedule(origin, reach, own_slot, rows):
    sub = lax.broadcasted_iota(jnp.int32, (rows, LANES), 0)
    lane = lax.broadcasted_iota(jnp.int32, (rows, LANES), 1)
    wanted = (origin <= sub) & (reach > sub)
    score = jnp.where(wanted, (reach * LANES + lane) * SLOTS, -1)
    ready = jnp.where(wanted & (origin == sub), score + own_slot, -1)
    later = jnp.where(origin == sub, -1, score)

    def step(carry, turn):
        ready, later, held, table, used = carry
        best = jnp.max(ready, axis=1, keepdims=True)
        chosen = (ready == best) & (best >= 0)
        table = jnp.where(lane == turn, jnp.where(best >= 0, best & (SLOTS - 1), -1), table)
        used = jnp.where(jnp.max(best, axis=0, keepdims=True) >= 0, turn + 1, used)
        passed = jnp.where(chosen, 1, 0)
        arrived = jnp.concatenate([jnp.zeros((1, LANES), jnp.int32), passed[:-1]], axis=0) > 0
        slot = OWN + turn
        ready = jnp.where(chosen, -1, ready)
        ready = jnp.where(arrived & (later >= 0), later + slot, ready)
        later = jnp.where(arrived, -1, later)
        return ready, later, jnp.where(arrived, slot, held), table, used

    start = jnp.zeros((rows, LANES), jnp.int32)
    return (ready, later, start, start - 1, jnp.zeros((1, 1), jnp.int32)), step


def route_kernel(sectors, where_ref, lists_ref, table_ref, count_ref):
    chips = sectors // 2
    rows = -(-chips // 8) * 8
    lane = lax.broadcasted_iota(jnp.int32, (1, LANES), 1)
    valid = lane < 2 * sectors
    block = lane % sectors
    origin = jnp.where(valid, block // 2, chips)
    own_slot = 2 * (lane // sectors) + block % 2
    reach = jnp.full((1, LANES), -1, jnp.int32)
    back = jnp.full((1, LANES), -1, jnp.int32)
    for k in range(sectors):
        asked = jnp.where(lane < sectors, lists_ref[0, 2 * k], lists_ref[0, 2 * k + 1])
        hit = (block == asked) & valid
        reach = jnp.where(hit, k // 2, reach)
        back = jnp.where(hit, jnp.maximum(back, chips - 1 - k // 2), back)
    right, right_step = schedule(origin, reach, own_slot, rows)
    mirrored = jnp.where(valid, chips - 1 - origin, chips)
    left, left_step = schedule(mirrored, back, own_slot, rows)

    def busy(carry):
        _, right, left = carry
        return jnp.maximum(jnp.max(right[0]), jnp.max(left[0])) >= 0

    def step(carry):
        turn, right, left = carry
        return turn + 1, right_step(right, turn), left_step(left, turn)

    carry = (jnp.int32(0), right, left)
    for _ in range(FIXED_ROUNDS):
        carry = step(carry)
    _, right, left = lax.while_loop(busy, step, carry)
    me = where_ref[0]
    chip = me // 2
    sub = lax.broadcasted_iota(jnp.int32, (rows, LANES), 0)

    def row(array, index):
        return jnp.sum(jnp.where(sub == index, array, 0), axis=0, keepdims=True)

    core = me % 2
    arrived = jnp.where(core == 0, row(right[2], chip), row(left[2], chips - 1 - chip))
    behind = ((chip - origin) * (1 - 2 * core) > 0) & valid
    ends = jnp.full((1, LANES), -1, jnp.int32)
    for at, owner in enumerate((me, me + 1 - 2 * core)):
        for kind in range(2):
            hit = lane == kind * sectors + lists_ref[0, 2 * owner + kind]
            slot = jnp.where(behind, arrived, -1)
            if at == 0:
                slot = jnp.where(origin == chip, own_slot, slot)
            slot = jnp.sum(jnp.where(hit, slot + 1, 0), axis=1, keepdims=True) - 1
            ends = jnp.where(lane == 2 * at + kind, slot, ends)
    sends = jnp.where(core == 0, row(right[3] + 1, chip), row(left[3] + 1, chips - 1 - chip)) - 1
    table_ref[...] = jnp.concatenate([sends, ends, jnp.zeros((6, LANES), jnp.int32)], axis=0)
    count_ref[...] = jnp.broadcast_to(jnp.maximum(right[4], left[4]), (8, LANES))


def fetches(slot, stream, core, target, sem, blocks, pieces, tail):
    share = target.shape[0]
    half = pl.ds(stream * share, share)
    sources = []
    for at, block in enumerate(blocks):
        kind, other = at % 2, at // 2
        seat = core if other == 0 else 1 - core
        sources.append((slot == 2 * kind + seat, block.at[half]))
    for at, piece in enumerate(pieces):
        sources.append((slot == OWN + at, piece))
    if tail is not None:
        base = OWN + FIXED_ROUNDS
        sources.append((slot >= base, tail.at[jnp.clip(slot - base, 0, tail.shape[0] - 1)]))
    return [(use, pltpu.make_async_copy(source, target, sem)) for use, source in sources]


def run_copies(copies, verb):
    for use, copy in copies:

        @pl.when(use)
        def _(copy=copy):
            getattr(copy, verb)()


def stage_kernel(stream, has_tail, turn_ref, where_ref, table_ref, *refs):
    blocks, pieces, (out_ref, sem) = refs[:4], list(refs[4:-2]), refs[-2:]
    tail = pieces.pop() if has_tail else None
    slot = table_ref[0, turn_ref[0]]
    copies = fetches(slot, stream, where_ref[0] % 2, out_ref, sem.at[0], blocks, pieces, tail)
    run_copies(copies, "start")
    run_copies(copies, "wait")


def held_copies(kind, at, where_ref, table_ref, pieces, target, sems):
    blocks, pieces, tails = pieces[:4], pieces[4:-STREAMS], pieces[-STREAMS:]
    share = target.shape[0] // STREAMS
    copies = []
    for stream in range(STREAMS):
        copies += fetches(
            table_ref[1, 2 * at + kind],
            stream,
            where_ref[0] % 2,
            target.at[pl.ds(stream * share, share)],
            sems.at[kind * STREAMS + stream],
            blocks,
            pieces[stream * FIXED_ROUNDS : (stream + 1) * FIXED_ROUNDS],
            tails[stream],
        )
    return copies


def last_kernel(where_ref, table_ref, *refs):
    pieces, (out_ref, sems) = refs[:-2], refs[-2:]
    copies = []
    for kind in range(2):
        copies += held_copies(kind, 1, where_ref, table_ref, pieces, out_ref.at[kind], sems)
    run_copies(copies, "start")
    run_copies(copies, "wait")


def small_product(a, b):
    total = a[:, 0:1] * b[0:1, :]
    for k in range(1, 8):
        total = total + a[:, k : k + 1] * b[k : k + 1, :]
    return total


def finish_kernel(entries, me_ref, all_ref, basis_ref, state_ref, hess_ref):
    f32 = jnp.float32
    count = basis_ref.shape[0]
    sectors = all_ref.shape[0]
    data = all_ref[...]
    if sectors < LANES:
        data = jnp.concatenate([data, jnp.zeros((LANES - sectors, LANES), f32)], axis=0)
    data = data.T
    width = data.shape[1]
    sub = lax.broadcasted_iota(jnp.int32, (8, width), 0)
    lane = lax.broadcasted_iota(jnp.int32, (8, width), 1)
    start = data[7:8, :]
    moves = [data[8 * j : 8 * j + 8, :] for j in range(count)]
    moves[0] = jnp.where(sub == 7, 0.0, moves[0])
    grams = [data[64 + 8 * j : 64 + 8 * j + 8, :] for j in range(count)]

    def combine(columns, x, upto=count):
        total = columns[0] * x[0:1, :]
        for b in range(1, upto):
            total = total + columns[b] * x[b : b + 1, :]
        return total

    inner = [combine(grams, moves[j]) for j in range(count - 1)] + [moves[count - 1]]
    start_sq = jnp.sum(start * start * grams[0][0:1, :], axis=1, keepdims=True)
    basis = [jnp.where(sub == 0, start / jnp.sqrt(start_sq + EPS), 0.0)]
    hess = jnp.zeros((8, width), f32)
    for t in range(count):
        seen = combine(inner, basis[t], t + 1)
        stacked = jnp.zeros((8, width), f32)
        for s in range(t + 1):
            stacked = jnp.where(sub == s, jnp.sum(basis[s] * seen, axis=0, keepdims=True), stacked)
        h = jnp.sum(stacked, axis=1, keepdims=True)
        hess = jnp.where((lane == t) & (sub <= t), h, hess)
        if t + 1 < count:
            rest = combine(moves, basis[t], t + 1)
            for s in range(t + 1):
                rest = rest - h[s : s + 1, :] * basis[s]
            rest_sq = jnp.sum(rest * combine(grams, rest), keepdims=True)
            beta = jnp.sqrt(jnp.maximum(rest_sq, 0.0) + EPS)
            hess = jnp.where((lane == t) & (sub == t + 1), beta, hess)
            basis.append(rest / beta)
    hess_ref[...] = hess[:, :count]

    scaled = -TAU / 16.0 * hess
    term = jnp.where((sub == lane), 1.0, 0.0)
    series = term
    for order in range(1, 11):
        term = small_product(term, scaled) / float(order)
        series = series + term
    for square in range(4):
        series = small_product(series, series)
    coefficients = series[:, 0:1]
    norm = jnp.sum(coefficients * coefficients, axis=0, keepdims=True)
    rescale = jnp.sqrt(jnp.float32(entries)) / jnp.sqrt(norm)
    mine = jnp.zeros((8, width), f32)
    for t in range(count):
        mine = mine + coefficients[t : t + 1, :] * basis[t]
    mine = jnp.sum(jnp.where(lane == me_ref[0], mine, 0.0), axis=1, keepdims=True) * rescale
    step = 64
    for at in range(0, state_ref.shape[0], step):
        total = mine[0:1, :] * basis_ref[0, at : at + step, :]
        for i in range(1, count):
            total = total + mine[i : i + 1, :] * basis_ref[i, at : at + step, :]
        state_ref[at : at + step, :] = total


def shifted(x, step):
    group = lax.axis_size("group")
    return lax.ppermute(x, "group", [((k + step) % group, k) for k in range(group)])


def fetch_blocks(left_env, right_env, lists, mixing, sectors, me):
    channels, size = left_env.shape[0], left_env.shape[1]
    share = channels // STREAMS
    bf16 = left_env.dtype
    small = pl.BlockSpec(memory_space=pltpu.SMEM)
    whole = pl.BlockSpec(memory_space=pltpu.VMEM)
    place = pl.BlockSpec(memory_space=pl.ANY)
    swap = [(k, k + 1 - 2 * (k % 2)) for k in range(sectors)]
    along = [(k, k + 2) for k in range(0, sectors - 2, 2)]
    along += [(k, k - 2) for k in range(3, sectors, 2)]

    def pieces_of(*lead):
        return jax.ShapeDtypeStruct(lead + (share, size, size), bf16)

    where = me.reshape(1)
    blocks = [left_env, right_env] + [
        lax.ppermute(env, "sector", swap) for env in (left_env, right_env)
    ]
    table, count = pl.pallas_call(
        lambda *refs: route_kernel(sectors, *refs),
        out_shape=(jax.ShapeDtypeStruct((8, LANES), jnp.int32),) * 2,
        in_specs=[small, small],
        out_specs=(whole, whole),
        name="route",
    )(where, lists)
    rounds = spread_rows(count, "group", jnp.maximum, lax.pmax)[0, 0]

    def stage(stream, turn, held, tail=None):
        inputs = blocks + held + ([] if tail is None else [tail])
        return pl.pallas_call(
            lambda *refs: stage_kernel(stream, tail is not None, *refs),
            out_shape=pieces_of(),
            in_specs=[small] * 3 + [place] * len(inputs),
            out_specs=whole,
            scratch_shapes=[pltpu.SemaphoreType.DMA((1,))],
            name="stage",
        )(jnp.asarray(turn, jnp.int32).reshape(1), where, table, *inputs)

    held = [[] for _ in range(STREAMS)]
    for turn in range(FIXED_ROUNDS):
        for stream in range(STREAMS):
            flow = stage(stream, turn, held[stream])
            if (turn, stream) == (2, 0):
                flow, mixing = lax.optimization_barrier((flow, mixing))
            held[stream] = held[stream] + [lax.ppermute(flow, "sector", along)]

    def more(carry):
        return carry[0] < rounds

    def again(carry):
        turn, tails = carry
        moved = [
            lax.ppermute(stage(stream, turn, held[stream], tails[stream]), "sector", along)
            for stream in range(STREAMS)
        ]
        tails = [
            lax.dynamic_update_slice_in_dim(tail, piece[None], turn - FIXED_ROUNDS, axis=0)
            for tail, piece in zip(tails, moved)
        ]
        return turn + 1, tails

    room = pl.pallas_call(
        lambda *refs: None,
        out_shape=tuple(pieces_of(TAIL_ROUNDS) for _ in range(STREAMS)),
        out_specs=tuple(place for _ in range(STREAMS)),
        name="room",
    )()
    _, tails = lax.while_loop(more, again, (jnp.int32(FIXED_ROUNDS), list(room)))

    pieces = blocks + [piece for each in held for piece in each] + tails
    theirs = pl.pallas_call(
        last_kernel,
        out_shape=jax.ShapeDtypeStruct((2, channels, size, size), bf16),
        in_specs=[small] * 2 + [place] * len(pieces),
        out_specs=whole,
        scratch_shapes=[pltpu.SemaphoreType.DMA((2 * STREAMS,))],
        name="last",
    )(where, table, *pieces)
    return table, mixing, lax.ppermute(theirs, "sector", swap), pieces


def spread_blocks(left_env, right_env, lists, sectors):
    channels, size = left_env.shape[0], left_env.shape[1]
    sides = []
    for side, env in enumerate((left_env, right_env)):
        pieces = env.reshape(sectors, channels // sectors, size, size)
        spread = lax.all_to_all(pieces, "sector", split_axis=0, concat_axis=0, tiled=True)
        sends = jnp.take(spread, lists[0, side : 2 * sectors : 2], axis=0, mode="clip")
        sides.append(
            lax.all_to_all(sends, "sector", split_axis=0, concat_axis=0, tiled=True).reshape(
                channels, size, size
            )
        )
    return jnp.stack(sides)


def local(state, panel, left_env, right_env, left_match, right_match, phys_states):
    _, size, phys, _ = state.shape
    channels = left_env.shape[1]
    sector_count = lax.axis_size("sector")
    seat = lax.axis_index("sector").astype(jnp.int32)

    lane = lax.broadcasted_iota(jnp.int32, (8, LANES), 1)
    lists = jnp.where(lane == 2 * seat + 1, right_match, -1)
    lists = jnp.where(lane == 2 * seat, left_match, lists)
    lists = spread_rows(lists, "sector", jnp.maximum, lax.pmax)

    slices = [panel] + [shifted(panel, step) for step in range(1, lax.axis_size("group"))]
    mixing = arrange_mix(select_mix(slices, phys_states[0]), panel.shape[0])
    if sector_count <= 2 * LINE:
        table, mixing, theirs, pieces = fetch_blocks(
            left_env[0], right_env[0], lists, mixing, sector_count, seat
        )
    else:
        theirs, pieces = spread_blocks(left_env[0], right_env[0], lists, sector_count), []
        table = jnp.full((8, LANES), -1, jnp.int32)

    whole = pl.BlockSpec(memory_space=pltpu.VMEM)
    rows, f32, bf16 = size * phys, jnp.float32, jnp.bfloat16
    small = pl.BlockSpec(memory_space=pltpu.SMEM)
    place = pl.BlockSpec(memory_space=pl.ANY)
    devices = lax.axis_size("group") * sector_count
    me = (lax.axis_index("group").astype(jnp.int32) * sector_count + seat).reshape(1)
    basis, stats = pl.pallas_call(
        krylov_kernel,
        out_shape=(
            jax.ShapeDtypeStruct((KRYLOV, rows, size), f32),
            jax.ShapeDtypeStruct((devices, LANES), f32),
        ),
        in_specs=[small] * 2 + [whole] * 3 + [place] * len(pieces),
        out_specs=(whole, whole),
        scratch_shapes=[
            pltpu.VMEM((2, channels, size, size), bf16),
            pltpu.VMEM((channels * size, size), f32),
            pltpu.VMEM((channels * size, size), bf16),
            pltpu.VMEM((channels * size, size), bf16),
            pltpu.VMEM((size, rows), bf16),
            pltpu.VMEM((rows, channels * size), bf16),
            pltpu.VMEM((rows, size), f32),
            pltpu.SemaphoreType.DMA((2 * STREAMS,)),
        ],
        compiler_params=pltpu.CompilerParams(vmem_limit_bytes=40 * 1024 * 1024),
        name="krylov",
    )(table, me, state.reshape(rows, size), mixing, theirs, *pieces)

    gathered = spread_rows(stats, "sector", jnp.add, lax.psum)
    gathered = spread_rows(gathered, "group", jnp.add, lax.psum)
    entries = rows * size * devices
    evolved, hessenberg = pl.pallas_call(
        lambda *refs: finish_kernel(entries, *refs),
        out_shape=(
            jax.ShapeDtypeStruct((rows, size), f32),
            jax.ShapeDtypeStruct((KRYLOV, KRYLOV), f32),
        ),
        in_specs=[small, whole, whole],
        out_specs=(whole, whole),
        compiler_params=pltpu.CompilerParams(vmem_limit_bytes=24 * 1024 * 1024),
        name="finish",
    )(me, gathered, basis)
    return (evolved.reshape(state.shape), hessenberg)


def solution(mesh):
    return jax.shard_map(
        local,
        mesh=mesh,
        in_specs=(
            P(("group", "sector"), None, None, None),
            P("group", None, None),
            P(("group", "sector"), None, None, None),
            P(("group", "sector"), None, None, None),
            P(("group", "sector")),
            P(("group", "sector")),
            P(("group", "sector"), None),
        ),
        out_specs=(P(("group", "sector"), None, None, None), P()),
        check_vma=False,
    )
```
